32 devices in a mesh: section: 8 (over z, core), fsdp: 4 (over y, x).
Axes of the slice: x: 2, y: 2, z: 4, core: 2. Of those that a mesh axis runs over, the one named last changes fastest.
Arguments:
- tokens: bfloat16 [8, 512, 5120], P('section', 'fsdp'), may hold values from -60 to 60
- cotangents: bfloat16 [8, 512, 1024], P('section', 'fsdp'), may hold values from -6 to 6
- norm_gain: float32 [8, 5120], P('section'), may hold values from 0.1 to 1.9
- master: float32 [8, 5120, 1024], P('section', 'fsdp'), may hold values from -5 to 5
- moment: float32 [8, 5120, 1024], P('section', 'fsdp'), may hold values from -4 to 4
- second: float32 [8, 5120, 1024], P('section', 'fsdp'), may hold values from 0.05 to 2
- head_owner: int32 [8, 4], P('section'), may hold values from 0 to 3, each once within a row
- plan: int32 [4], replicated, may hold values from 0 to 3, each once
Outputs:
- input_grads: bfloat16 [8, 512, 5120], P('section', 'fsdp')
- moment_new: float32 [8, 5120, 1024], P('section', 'fsdp')
- second_new: float32 [8, 5120, 1024], P('section', 'fsdp')
- rollout: bfloat16 [8, 1024, 5120], P('section', 'fsdp')
The draws below stay inside these ranges and needn't reach their ends.
Inputs may be any that keep to these rules, and one draw needn't show every extreme that they name: `head_owner`: each row lists every head once. `plan`: every slot is named once.
All inputs are finite; a program needn't handle non-finite values.
Results may differ from the reference program's by a relative error of at most 0.011.
Values may be sent and summed in bfloat16 or wider, within the bound.
No kernel may reach another device: no remote copies, remote signals or barrier semaphores. Data moves between devices by JAX's collectives and lax.ppermute only.
A program may use at most 192 MiB of HBM per device.

```python
import math
import jax
import jax.numpy as jnp
from jax import lax

D = 5120
HEAD = 128
KV_HEADS = 4
MICRO = 4
TOK_DEV = 128
KVC = 1024
TOKENS = 512
LAYERS = 8
N_FSDP = 4


def draw_tokens(key, part):
    key = jax.random.fold_in(key, 11)
    base_key, row_key, col_key = jax.random.split(key, 3)
    raw_values = jnp.clip(jax.random.normal(base_key, (LAYERS, TOKENS, D), jnp.float32), -5.0, 5.0)
    row_scale = jnp.exp(jax.random.uniform(row_key, (LAYERS, TOKENS, 1), jnp.float32, 0.0, math.log(10.0))) * 0.4
    col_scale = jnp.exp(jax.random.uniform(col_key, (LAYERS, 1, D), jnp.float32, 0.0, math.log(10.0))) * 0.3
    return (raw_values * row_scale * col_scale).astype(jnp.bfloat16)


def level_of(stream_key, extent, cuts, low, top_value):
    def one(position, parts):
        steps = jax.random.uniform(jax.random.fold_in(jax.random.fold_in(stream_key, 6), position), (parts,), jnp.float32, low / len(cuts), top_value / len(cuts))
        return jnp.repeat(jnp.exp(steps), extent[position] // parts).reshape((-1,) + (1,) * (len(extent) - position - 1))

    gain = one(*cuts[0])
    for cut in cuts[1:]:
        gain = gain * one(*cut)
    return gain


def scatter_about(key, dims, scale, reach, pieces=(), kind=jnp.bfloat16):
    loudness = level_of(key, dims, pieces, -0.22, 0.18) if pieces else 1.0
    drawn = jax.random.normal(key, dims, jnp.float32) * scale * loudness
    return jnp.minimum(jnp.maximum(drawn, -reach), reach).astype(kind)


def setup_inputs(seed: int = 0) -> dict:
    keys = jax.random.split(jax.random.key(seed), 9)
    tokens = draw_tokens(jax.random.fold_in(keys[8], 71), 0)
    cotangents = scatter_about(keys[1], (LAYERS, TOKENS, KVC), 1.0, 6.0, ((0, 8), (1, 4)))
    norm_gain = jnp.clip(1.0 + 0.18 * jax.random.normal(keys[2], (LAYERS, D), jnp.float32), 0.1, 1.9)
    master = scatter_about(keys[3], (LAYERS, D, KVC), 1.0, 5.0, ((0, 8), (1, 4)), jnp.float32)
    moment = scatter_about(keys[4], (LAYERS, D, KVC), 0.3, 4.0, ((0, 8), (1, 4)), jnp.float32)
    second = jnp.clip(jnp.exp(math.log(2.0) - 3.6888794 * jax.random.uniform(keys[5], (LAYERS, D, KVC), jnp.float32) ** level_of(keys[5], (LAYERS, D, KVC), ((0, 8), (1, 4)), -0.2, 0.2)), 0.05, 2.0)
    head_owner = jax.vmap(lambda own: jax.random.permutation(own, KV_HEADS))(jax.random.split(keys[6], LAYERS)).reshape((LAYERS, KV_HEADS)).astype(jnp.int32)
    plan = jax.random.permutation(keys[7], MICRO).astype(jnp.int32)
    return {"tokens": tokens, "cotangents": cotangents, "norm_gain": norm_gain, "master": master, "moment": moment, "second": second, "head_owner": head_owner, "plan": plan}


beta_one = 0.9
beta_two = 0.95
bias_one = 1.0 - 0.9 ** 10
bias_two = 1.0 - 0.95 ** 10
adam_eps = 1e-08
learn_rate = 0.02
weight_decay = 0.1
norm_eps = 1e-06

def input_term(widened, inverse, gain_row, spread):
    scaled = spread * gain_row
    mean_term = lax.optimization_barrier(jnp.mean(scaled * widened, axis=-1, keepdims=True))
    return inverse * scaled - widened * inverse * inverse * inverse * mean_term

def adam_step(master, moment, second, gradient):
    moment_new = beta_one * moment + (1.0 - beta_one) * gradient
    second_new = beta_two * second + (1.0 - beta_two) * gradient * gradient
    update = moment_new / bias_one / (jnp.sqrt(second_new / bias_two) + adam_eps)
    weights = master - learn_rate * (update + weight_decay * master)
    return (moment_new, second_new, weights)

def reference(tokens, cotangents, norm_gain, master, moment, second, head_owner, plan):
    proj_scale = D ** (-0.5)

    def one_layer(running, layer_items):
        tok_rows, cot_rows, gain_row, master_rows, moment_rows, second_rows, owner_row = layer_items
        blocks = cot_rows.reshape(N_FSDP, MICRO, TOK_DEV // MICRO, KVC)
        ordered = jnp.take(blocks, plan, axis=1).reshape(TOKENS, KVC)
        widened = tok_rows.astype(jnp.float32)
        inverse = lax.rsqrt(lax.optimization_barrier(jnp.mean(widened * widened, axis=-1, keepdims=True)) + norm_eps)
        normed = (widened * inverse * gain_row).astype(jnp.bfloat16)
        low_weights = master_rows.astype(jnp.bfloat16)
        spread = jnp.dot(ordered, low_weights.T, preferred_element_type=jnp.float32) * proj_scale
        own_term = input_term(widened, inverse, gain_row, spread)

        def shard_grad(running_grad, shard_pair):
            normed_shard, cot_shard = shard_pair
            partial_term = jnp.dot(normed_shard.T, cot_shard, preferred_element_type=jnp.float32) * proj_scale
            rounded = lax.optimization_barrier(partial_term.astype(jnp.bfloat16))
            return (running_grad + rounded.astype(jnp.float32), None)
        gradient, _ = lax.scan(shard_grad, jnp.zeros((D, KVC), jnp.float32), (normed.reshape(N_FSDP, TOK_DEV, D), ordered.reshape(N_FSDP, TOK_DEV, KVC)))
        moment_new, second_new, weights = adam_step(master_rows, moment_rows, second_rows, gradient)
        by_head = weights.astype(jnp.bfloat16).reshape(D, 2, KV_HEADS, HEAD)
        placed = jnp.take(by_head, owner_row, axis=2)
        rollout = jnp.transpose(placed, (2, 1, 3, 0)).reshape(KVC, D)
        summed = running + own_term
        return (summed, (summed.astype(jnp.bfloat16), moment_new, second_new, rollout))
    _, outputs = lax.scan(one_layer, jnp.zeros((TOKENS, D), jnp.float32), (tokens, cotangents, norm_gain, master, moment, second, head_owner), reverse=True)
    return (outputs[0], outputs[1], outputs[2], outputs[3])
```

```python
import functools

import jax
import jax.numpy as jnp
from jax import lax
from jax.experimental import pallas as pl
from jax.experimental.pallas import tpu as pltpu
from jax.sharding import PartitionSpec as P

beta_one = 0.9
beta_two = 0.95
bias_one = 1.0 - 0.9**10
bias_two = 1.0 - 0.95**10
adam_eps = 1e-08
learn_rate = 0.02
weight_decay = 0.1
norm_eps = 1e-06

bf16 = jnp.bfloat16
f32 = jnp.float32


def swap(x, axis, k):
    count = lax.axis_size(axis)
    return lax.ppermute(x, axis, [(i, i ^ k) for i in range(count)])


def adam_step(master, moment, second, gradient):
    moment_new = beta_one * moment + (1.0 - beta_one) * gradient
    second_new = beta_two * second + (1.0 - beta_two) * gradient * gradient
    update = moment_new / bias_one / (jnp.sqrt(second_new / bias_two) + adam_eps)
    weights = master - learn_rate * (update + weight_decay * master)
    return (moment_new, second_new, weights)


def plan_rows(cot_rows, plan):
    micro_count = plan.shape[0]
    blocks = cot_rows.reshape(micro_count, -1, cot_rows.shape[-1])
    return jnp.take(blocks, plan, axis=0).reshape(cot_rows.shape)


def suffix_sum(own_term, axis):
    count = lax.axis_size(axis)
    place = lax.axis_index(axis)
    low = own_term.astype(bf16)
    pair = lax.ppermute(low, axis, [(i + 1, i) for i in range(0, count, 2)])
    total = own_term + pair.astype(f32)
    above = jnp.zeros_like(low)
    for z in range(count // 2 - 1, 0, -1):
        got = lax.ppermute(total.astype(bf16), axis, [(2 * z, 2 * z - 2)])
        total = total + got.astype(f32)
        above = above + got
    from_pair = lax.ppermute(above, axis, [(i, i + 1) for i in range(0, count, 2)])
    return jnp.where(place % 2 == 0, total, own_term + from_pair.astype(f32))


def shards_any(tokens, cotangents, norm_gain, master, moment, second, head_owner, plan):
    tok_rows = tokens[0]
    gain_row = norm_gain[0]
    master_rows = master[0]
    owner_row = head_owner[0]
    width = tok_rows.shape[1]
    tok_count = tok_rows.shape[0]
    proj_scale = width ** (-0.5)
    count = lax.axis_size("fsdp")
    place = lax.axis_index("fsdp")
    cols = width // count

    def block_of(x, k):
        return lax.dynamic_slice_in_dim(x, (place ^ k) * cols, cols, axis=-1)

    ordered = plan_rows(cotangents[0], plan)
    all_ordered = [ordered] + [swap(ordered, "fsdp", k) for k in range(1, count)]
    widened = tok_rows.astype(f32)
    inverse = lax.rsqrt(jnp.mean(widened * widened, axis=-1, keepdims=True) + norm_eps)
    normed = (widened * inverse * gain_row).astype(bf16)
    all_normed = [block_of(normed, 0)] + [
        swap(block_of(normed, k), "fsdp", k) for k in range(1, count)
    ]
    low_weights = master_rows.astype(bf16)
    spread = []
    for k in range(count):
        part = (
            jnp.einsum("tc,rc->tr", all_ordered[k], low_weights, preferred_element_type=f32)
            * proj_scale
        )
        spread.append(part if k == 0 else swap(part.astype(bf16), "fsdp", k).astype(f32))

    gradient = (
        jnp.einsum(
            "td,tc->dc",
            jnp.concatenate(all_normed, axis=0),
            jnp.concatenate(all_ordered, axis=0),
            preferred_element_type=f32,
        )
        * proj_scale
    )
    moment_new, second_new, weights = adam_step(master_rows, moment[0], second[0], gradient)
    heads = owner_row.shape[0]
    low_new = weights.astype(bf16).reshape(cols, 2, heads, -1)
    arranged = jnp.take(low_new, owner_row, axis=2).transpose(2, 1, 3, 0).reshape(count, -1, cols)
    rollout = jnp.zeros((arranged.shape[1], width), bf16)
    for k in range(count):
        part = lax.dynamic_index_in_dim(arranged, place ^ k, 0, False)
        if k:
            part = swap(part, "fsdp", k)
        rollout = lax.dynamic_update_slice_in_dim(rollout, part, (place ^ k) * cols, axis=1)

    tok_k = [block_of(tok_rows, k).astype(f32) for k in range(count)]
    scaled = [spread[k] * block_of(gain_row, k) for k in range(count)]
    mean_term = sum(jnp.sum(scaled[k] * tok_k[k], axis=-1, keepdims=True) for k in range(count)) / width
    factor = inverse * inverse * inverse * mean_term
    own_term = jnp.concatenate(
        [inverse * scaled[k] - tok_k[k] * factor for k in range(count)], axis=0
    )
    summed = suffix_sum(own_term, "section").astype(bf16).reshape(count, tok_count, cols)
    input_grads = jnp.zeros((tok_count, width), bf16)
    for k in range(count):
        input_grads = lax.dynamic_update_slice_in_dim(
            input_grads, summed[k], (place ^ k) * cols, axis=1
        )
    return (input_grads[None], moment_new[None], second_new[None], rollout[None])


def call(name, body, grid, prefetch, in_specs, out_specs, out_shape, scratch=(), aliases=None, vmem=24, work=1):
    return pl.pallas_call(
        body,
        grid_spec=pltpu.PrefetchScalarGridSpec(
            num_scalar_prefetch=prefetch,
            grid=grid,
            in_specs=in_specs,
            out_specs=out_specs,
            scratch_shapes=list(scratch),
        ),
        out_shape=out_shape,
        input_output_aliases=aliases or {},
        name=name,
        compiler_params=pltpu.CompilerParams(
            vmem_limit_bytes=vmem * 1024 * 1024,
            dimension_semantics=("arbitrary",) * len(grid),
        ),
        cost_estimate=pl.CostEstimate(flops=work, bytes_accessed=1, transcendentals=0),
    )


def whole(shape):
    return pl.BlockSpec(shape, lambda *_: (0,) * len(shape))


def part_of(place, k, cols):
    return pl.ds(pl.multiple_of((place ^ k) * cols, 128), cols)


def prep_body(count, place_ref, tok_ref, gain_ref, inv_ref, *out_refs):
    place = place_ref[0]
    width = tok_ref.shape[1]
    cols = width // count
    total = jnp.zeros((tok_ref.shape[0], 1), f32)
    for k in range(count):
        x = tok_ref[:, k * cols : (k + 1) * cols].astype(f32)
        total = total + jnp.sum(x * x, axis=-1, keepdims=True)
    inverse = lax.rsqrt(total / width + norm_eps)
    inv_ref[...] = inverse
    for k in range(count):
        part = part_of(place, k, cols)
        x = tok_ref[:, part].astype(f32)
        out_refs[k][...] = (x * inverse * gain_ref[:, part]).astype(bf16).T


def low_body(master_ref, _, low_ref):
    low_ref[...] = master_ref[...].astype(bf16)


def spread_body(count, micro, scale, plan_ref, *refs):
    cots, (low_ref, ordered_ref), outs = refs[:count], refs[count : count + 2], refs[count + 2 :]
    rows = cots[0].shape[0]
    size = rows // micro
    for k in range(count):
        for i in range(micro):
            at = pl.multiple_of(plan_ref[i] * size, size)
            ordered_ref[k * rows + i * size : k * rows + (i + 1) * size, :] = cots[k][
                pl.ds(at, size), :
            ]
    step = 256
    for at in range(0, low_ref.shape[0], step):
        product = lax.dot_general(
            ordered_ref[...],
            low_ref[at : at + step, :],
            (((1,), (1,)), ((), ())),
            preferred_element_type=f32,
        )
        for k in range(count):
            outs[k][:, at : at + step] = (product[k * rows : (k + 1) * rows, :] * scale).astype(bf16)


def grad_body(count, head, scale, place_ref, owner_ref, *refs):
    normed, refs = refs[:count], refs[count:]
    ordered_ref, master_ref, moment_ref, second_ref, moment_out, second_out = refs[:6]
    outs, mark_ref, joined, fresh = refs[6 : 6 + count], *refs[6 + count :]
    tok_count = normed[0].shape[1]
    kv_cols = master_ref.shape[1]
    mark_ref[...] = jnp.zeros_like(mark_ref)
    for k in range(count):
        joined[:, k * tok_count : (k + 1) * tok_count] = normed[k][...]
    step = 256
    size = joined.shape[0]
    rows = pl.ds(pl.multiple_of(pl.program_id(0) * size, size), size)
    for at in range(0, kv_cols, step):
        here = slice(at, at + step)
        part = jnp.dot(joined[...], ordered_ref[:, here], preferred_element_type=f32)
        moment_new = beta_one * moment_ref[rows, here] + ((1.0 - beta_one) * scale) * part
        second_new = beta_two * second_ref[rows, here] + (
            ((1.0 - beta_two) * scale * scale) * part
        ) * part
        moment_out[:, here] = moment_new
        second_out[:, here] = second_new
        scaled = second_new * (1.0 / bias_two)
        root = scaled * lax.rsqrt(scaled) + adam_eps
        weights = master_ref[rows, here] * (1.0 - learn_rate * weight_decay) - (
            moment_new * (learn_rate / bias_one)
        ) * pl.reciprocal(root, approx=True)
        fresh[:, here] = weights.astype(bf16)
    for k in range(count):
        owner = owner_ref[place_ref[0] ^ k] * head
        for p in range(2):
            lanes = pl.ds(pl.multiple_of(p * (kv_cols // 2) + owner, head), head)
            outs[k][p * head : (p + 1) * head, :] = fresh[:, lanes].T


def own_body(count, place_ref, core_ref, tok_ref, gain_ref, inv_ref, *refs):
    spread, (_, keep_ref, give_ref) = refs[:count], refs[count:]
    place = place_ref[0]
    core = core_ref[0]
    width = tok_ref.shape[1]
    cols = width // count
    half = tok_ref.shape[0] // 2
    for out_ref, pick in ((give_ref, 1 - core), (keep_ref, core)):
        rows = pl.ds(pl.multiple_of(pick * half, half), half)
        inverse = inv_ref[rows, :]
        total = jnp.zeros((half, 1), f32)
        for k in range(count):
            part = part_of(place, k, cols)
            scaled = spread[k][rows, :].astype(f32) * gain_ref[:, part]
            total = total + jnp.sum(
                scaled * tok_ref[rows, part].astype(f32), axis=-1, keepdims=True
            )
        factor = inverse * inverse * inverse * (total / width)
        for k in range(count):
            part = part_of(place, k, cols)
            scaled = spread[k][rows, :].astype(f32) * gain_ref[:, part]
            out_ref[:, part] = (
                inverse * scaled - tok_ref[rows, part].astype(f32) * factor
            ).astype(bf16)


def pair_body(chip_ref, keep_ref, got_ref, one_ref, two_ref):
    z = chip_ref[0]
    half = one_ref.shape[0]
    for out_ref, top in ((one_ref, z == 3), (two_ref, z == 2)):
        rows = pl.ds(pl.multiple_of(jnp.where(top, 0, half), half), half)
        out_ref[...] = (keep_ref[rows, :].astype(f32) + got_ref[rows, :].astype(f32)).astype(bf16)


def middle_body(chip_ref, keep_ref, got_ref, one_ref, two_ref, three_ref, four_ref):
    z = chip_ref[0]
    half = one_ref.shape[0]
    rows = pl.ds(pl.multiple_of(jnp.where(z == 2, half, 0), half), half)
    one = one_ref[...].astype(f32)
    two = two_ref[...].astype(f32)
    mine = keep_ref[rows, :].astype(f32) + got_ref[rows, :].astype(f32) + two
    three_ref[...] = (mine + jnp.where(z == 1, one, 0.0)).astype(bf16)
    four_ref[...] = (mine + one).astype(bf16)


def last_body(chip_ref, core_ref, keep_ref, got_ref, one_ref, two_ref, three_ref, four_ref, _, out_ref, send_ref):
    z = chip_ref[0]
    core = core_ref[0]
    half = one_ref.shape[0]
    for part in range(2):
        rows = slice(part * half, (part + 1) * half)
        one = one_ref[...].astype(f32)
        two = two_ref[...].astype(f32)
        three = three_ref[...].astype(f32)
        if part == 0:
            above = jnp.where(z == 1, one + two, three)
        else:
            four = four_ref[...].astype(f32)
            above = jnp.where(z == 0, four, jnp.where(z == 1, three, two))
        keep = keep_ref[rows, :].astype(f32)
        got = got_ref[rows, :].astype(f32)
        both = keep + got + above
        out_ref[rows, :] = jnp.where(core == 0, both, keep + above).astype(bf16)
        send_ref[rows, :] = jnp.where(core == 0, got + above, both).astype(bf16)


def place_body(place_ref, part_ref, *refs):
    refs[-1][...] = part_ref[...]


def marked_body(place_ref, part_ref, _, out_ref, mark_ref):
    out_ref[...] = part_ref[...]
    mark_ref[...] = jnp.zeros_like(mark_ref)


def shards(tokens, cotangents, norm_gain, master, moment, second, head_owner, plan):
    tok_rows, cot_rows = tokens[0], cotangents[0]
    master_rows, moment_rows, second_rows = master[0], moment[0], second[0]
    tok_count, width = tok_rows.shape
    kv_cols = cot_rows.shape[1]
    heads = head_owner.shape[1]
    head = kv_cols // (2 * heads)
    scale = width ** (-0.5)
    count = lax.axis_size("fsdp")
    place = lax.axis_index("fsdp").astype(jnp.int32)[None]
    section = lax.axis_index("section").astype(jnp.int32)
    core, chip = (section & 1)[None], (section >> 1)[None]
    cols = width // count
    half = tok_count // 2
    sds = jax.ShapeDtypeStruct
    dests = range(1, count)
    anywhere = pl.BlockSpec(memory_space=pl.ANY)
    mark = sds((8, 128), f32)

    cots = [cot_rows] + [swap(cot_rows, "fsdp", k) for k in dests]

    inverse, *normed = call(
        "prep",
        functools.partial(prep_body, count),
        (1,),
        1,
        [whole((tok_count, width)), whole((1, width))],
        [whole((tok_count, 1))] + [whole((cols, tok_count))] * count,
        [sds((tok_count, 1), f32)] + [sds((cols, tok_count), bf16)] * count,
    )(place, tok_rows, norm_gain)
    normed = [normed[0]] + [swap(normed[k], "fsdp", k) for k in dests]

    rows_step = 256
    low = call(
        "low",
        low_body,
        (cols // rows_step,),
        0,
        [pl.BlockSpec((rows_step, kv_cols), lambda i: (i, 0)), anywhere],
        pl.BlockSpec((rows_step, kv_cols), lambda i: (i, 0)),
        sds((cols, kv_cols), bf16),
    )(master_rows, inverse)
    ordered, *spread = call(
        "spread",
        functools.partial(spread_body, count, plan.shape[0], scale),
        (1,),
        1,
        [whole((tok_count, kv_cols))] * count + [whole((cols, kv_cols))],
        [whole((count * tok_count, kv_cols))] + [whole((tok_count, cols))] * count,
        [sds((count * tok_count, kv_cols), bf16)] + [sds((tok_count, cols), bf16)] * count,
        work=10**10,
    )(plan, *cots, low)
    spread = [spread[0]] + [swap(spread[k], "fsdp", k) for k in dests]

    state = pl.BlockSpec((rows_step, kv_cols), lambda i, *_: (i, 0))
    resident = pl.BlockSpec(memory_space=pltpu.VMEM)
    moment_new, second_new, *rollout_parts, grad_mark = call(
        "grad",
        functools.partial(grad_body, count, head, scale),
        (cols // rows_step,),
        2,
        [pl.BlockSpec((rows_step, tok_count), lambda i, *_: (i, 0))] * count
        + [resident, resident, resident, resident],
        [state, state]
        + [pl.BlockSpec((2 * head, rows_step), lambda i, *_: (0, i))] * count
        + [whole((8, 128))],
        [sds((cols, kv_cols), f32)] * 2 + [sds((2 * head, cols), bf16)] * count + [mark],
        scratch=[
            pltpu.VMEM((rows_step, count * tok_count), bf16),
            pltpu.VMEM((rows_step, kv_cols), bf16),
        ],
        vmem=20,
    )(place, head_owner[0], *normed, ordered, master_rows, moment_rows, second_rows)

    rollout = ()
    rollout_mark = ()
    for k in (0, 3, 1, 2):
        part = swap(rollout_parts[k], "fsdp", k) if k else rollout_parts[k]
        final = k == 2
        rollout, *rollout_mark = call(
            "place",
            marked_body if final else place_body,
            (1,),
            1,
            [whole((2 * head, cols))] + ([anywhere] if k else []),
            [pl.BlockSpec((2 * head, cols), lambda i, place_ref, k=k: (0, place_ref[0] ^ k))]
            + ([whole((8, 128))] if final else []),
            [sds((2 * head, width), bf16)] + ([mark] if final else []),
            aliases={2: 0} if k else None,
            work=10**9,
        )(place, part, *([rollout] if k else []))

    keep, give = call(
        "own",
        functools.partial(own_body, count),
        (1,),
        2,
        [whole((tok_count, width)), whole((1, width)), whole((tok_count, 1))]
        + [whole((tok_count, cols))] * count
        + [anywhere],
        [whole((half, width))] * 2,
        [sds((half, width), bf16)] * 2,
    )(place, core, tok_rows, norm_gain, inverse, *spread, grad_mark)
    got = swap(give, "section", 1)

    def chips(pairs):
        return [(2 * a + c, 2 * b + c) for c in range(2) for a, b in pairs]

    quarter = half // 2
    full, part = whole((half, width)), whole((quarter, width))
    piece = sds((quarter, width), bf16)
    one, two = call("pair", pair_body, (1,), 1, [full, full], [part, part], [piece, piece])(
        chip, keep, got
    )
    one = lax.ppermute(one, "section", chips([(3, 1), (1, 2)]))
    two = lax.ppermute(two, "section", chips([(2, 1), (3, 2)]))
    three, four = call(
        "middle", middle_body, (1,), 1, [full, full, part, part], [part, part], [piece, piece]
    )(chip, keep, got, one, two)
    three = lax.ppermute(three, "section", chips([(1, 0), (2, 1), (3, 2)]))
    four = lax.ppermute(four, "section", chips([(2, 0)]))
    grads, send = call(
        "last",
        last_body,
        (1,),
        2,
        [full, full, part, part, part, part, anywhere],
        [pl.BlockSpec((half, width), lambda i, chip_ref, core_ref: (core_ref[0], 0)), full],
        [sds((tok_count, width), bf16), sds((half, width), bf16)],
    )(chip, core, keep, got, one, two, three, four, *rollout_mark)
    other = swap(send, "section", 1)
    grads = call(
        "join",
        place_body,
        (1,),
        1,
        [full, anywhere],
        pl.BlockSpec((half, width), lambda i, core_ref: (1 - core_ref[0], 0)),
        sds((tok_count, width), bf16),
        aliases={2: 0},
    )(core, other, grads)
    return (grads[None], moment_new[None], second_new[None], rollout[None])


def choose(*args):
    tokens, cotangents, norm_gain, master, moment, second, head_owner, plan = args
    count, sections = lax.axis_size("fsdp"), lax.axis_size("section")
    tok_count, width = tokens.shape[1:]
    kv_cols, heads = cotangents.shape[2], head_owner.shape[1]
    fits = (
        count == 4
        and sections == 8
        and heads == count
        and plan.shape[0] == 4
        and kv_cols == 2 * heads * 128
        and (width // count) % 256 == 0
        and tok_count % 128 == 0
        and tok_count % (16 * plan.shape[0]) == 0
    )
    return (shards if fits else shards_any)(*args)


def solution(mesh):
    in_specs = (
        P("section", "fsdp", None),
        P("section", "fsdp", None),
        P("section", None),
        P("section", "fsdp", None),
        P("section", "fsdp", None),
        P("section", "fsdp", None),
        P("section", None),
        P(),
    )
    out_specs = (
        P("section", "fsdp", None),
        P("section", "fsdp", None),
        P("section", "fsdp", None),
        P("section", "fsdp", None),
    )
    return jax.shard_map(choose, mesh=mesh, in_specs=in_specs, out_specs=out_specs, check_vma=False)
```

```python
import functools

import jax
import jax.numpy as jnp
from jax import lax
from jax.experimental import pallas as pl
from jax.experimental.pallas import tpu as pltpu
from jax.sharding import PartitionSpec as P

beta_one = 0.9
beta_two = 0.95
bias_one = 1.0 - 0.9**10
bias_two = 1.0 - 0.95**10
adam_eps = 1e-08
learn_rate = 0.02
weight_decay = 0.1
norm_eps = 1e-06

bf16 = jnp.bfloat16
f32 = jnp.float32


def swap(x, axis, k):
    count = lax.axis_size(axis)
    return lax.ppermute(x, axis, [(i, i ^ k) for i in range(count)])


def adam_step(master, moment, second, gradient):
    moment_new = beta_one * moment + (1.0 - beta_one) * gradient
    second_new = beta_two * second + (1.0 - beta_two) * gradient * gradient
    update = moment_new / bias_one / (jnp.sqrt(second_new / bias_two) + adam_eps)
    weights = master - learn_rate * (update + weight_decay * master)
    return (moment_new, second_new, weights)


def plan_rows(cot_rows, plan):
    micro_count = plan.shape[0]
    blocks = cot_rows.reshape(micro_count, -1, cot_rows.shape[-1])
    return jnp.take(blocks, plan, axis=0).reshape(cot_rows.shape)


def suffix_sum(own_term, axis):
    count = lax.axis_size(axis)
    place = lax.axis_index(axis)
    low = own_term.astype(bf16)
    pair = lax.ppermute(low, axis, [(i + 1, i) for i in range(0, count, 2)])
    total = own_term + pair.astype(f32)
    above = jnp.zeros_like(low)
    for z in range(count // 2 - 1, 0, -1):
        got = lax.ppermute(total.astype(bf16), axis, [(2 * z, 2 * z - 2)])
        total = total + got.astype(f32)
        above = above + got
    from_pair = lax.ppermute(above, axis, [(i, i + 1) for i in range(0, count, 2)])
    return jnp.where(place % 2 == 0, total, own_term + from_pair.astype(f32))


def shards_any(tokens, cotangents, norm_gain, master, moment, second, head_owner, plan):
    tok_rows = tokens[0]
    gain_row = norm_gain[0]
    master_rows = master[0]
    owner_row = head_owner[0]
    width = tok_rows.shape[1]
    tok_count = tok_rows.shape[0]
    proj_scale = width ** (-0.5)
    count = lax.axis_size("fsdp")
    place = lax.axis_index("fsdp")
    cols = width // count

    def block_of(x, k):
        return lax.dynamic_slice_in_dim(x, (place ^ k) * cols, cols, axis=-1)

    ordered = plan_rows(cotangents[0], plan)
    all_ordered = [ordered] + [swap(ordered, "fsdp", k) for k in range(1, count)]
    widened = tok_rows.astype(f32)
    inverse = lax.rsqrt(jnp.mean(widened * widened, axis=-1, keepdims=True) + norm_eps)
    normed = (widened * inverse * gain_row).astype(bf16)
    all_normed = [block_of(normed, 0)] + [
        swap(block_of(normed, k), "fsdp", k) for k in range(1, count)
    ]
    low_weights = master_rows.astype(bf16)
    spread = []
    for k in range(count):
        part = (
            jnp.einsum("tc,rc->tr", all_ordered[k], low_weights, preferred_element_type=f32)
            * proj_scale
        )
        spread.append(part if k == 0 else swap(part.astype(bf16), "fsdp", k).astype(f32))

    gradient = (
        jnp.einsum(
            "td,tc->dc",
            jnp.concatenate(all_normed, axis=0),
            jnp.concatenate(all_ordered, axis=0),
            preferred_element_type=f32,
        )
        * proj_scale
    )
    moment_new, second_new, weights = adam_step(master_rows, moment[0], second[0], gradient)
    heads = owner_row.shape[0]
    low_new = weights.astype(bf16).reshape(cols, 2, heads, -1)
    arranged = jnp.take(low_new, owner_row, axis=2).transpose(2, 1, 3, 0).reshape(count, -1, cols)
    rollout = jnp.zeros((arranged.shape[1], width), bf16)
    for k in range(count):
        part = lax.dynamic_index_in_dim(arranged, place ^ k, 0, False)
        if k:
            part = swap(part, "fsdp", k)
        rollout = lax.dynamic_update_slice_in_dim(rollout, part, (place ^ k) * cols, axis=1)

    tok_k = [block_of(tok_rows, k).astype(f32) for k in range(count)]
    scaled = [spread[k] * block_of(gain_row, k) for k in range(count)]
    mean_term = sum(jnp.sum(scaled[k] * tok_k[k], axis=-1, keepdims=True) for k in range(count)) / width
    factor = inverse * inverse * inverse * mean_term
    own_term = jnp.concatenate(
        [inverse * scaled[k] - tok_k[k] * factor for k in range(count)], axis=0
    )
    summed = suffix_sum(own_term, "section").astype(bf16).reshape(count, tok_count, cols)
    input_grads = jnp.zeros((tok_count, width), bf16)
    for k in range(count):
        input_grads = lax.dynamic_update_slice_in_dim(
            input_grads, summed[k], (place ^ k) * cols, axis=1
        )
    return (input_grads[None], moment_new[None], second_new[None], rollout[None])


def call(name, body, grid, prefetch, in_specs, out_specs, out_shape, scratch=(), aliases=None, vmem=16, work=1):
    return pl.pallas_call(
        body,
        grid_spec=pltpu.PrefetchScalarGridSpec(
            num_scalar_prefetch=prefetch,
            grid=grid,
            in_specs=in_specs,
            out_specs=out_specs,
            scratch_shapes=list(scratch),
        ),
        out_shape=out_shape,
        input_output_aliases=aliases or {},
        name=name,
        compiler_params=pltpu.CompilerParams(
            vmem_limit_bytes=vmem * 1024 * 1024,
            dimension_semantics=("arbitrary",) * len(grid),
        ),
        cost_estimate=pl.CostEstimate(flops=work, bytes_accessed=1, transcendentals=0),
    )


def whole(shape):
    return pl.BlockSpec(shape, lambda *_: (0,) * len(shape))


def part_of(place, k, cols):
    return pl.ds(pl.multiple_of((place ^ k) * cols, 128), cols)


def prep_body(count, place_ref, tok_ref, gain_ref, inv_ref, *out_refs):
    place = place_ref[0]
    width = tok_ref.shape[1]
    cols = width // count
    total = jnp.zeros((tok_ref.shape[0], 1), f32)
    for k in range(count):
        x = tok_ref[:, k * cols : (k + 1) * cols].astype(f32)
        total = total + jnp.sum(x * x, axis=-1, keepdims=True)
    inverse = lax.rsqrt(total / width + norm_eps)
    inv_ref[...] = inverse
    for k in range(count):
        part = part_of(place, k, cols)
        x = tok_ref[:, part].astype(f32)
        out_refs[k][...] = (x * inverse * gain_ref[:, part]).astype(bf16).T


def low_body(master_ref, moment_ref, _, master_out, moment_out, low_ref, sems):
    copies = [
        pltpu.make_async_copy(master_ref, master_out, sems.at[0]),
        pltpu.make_async_copy(moment_ref, moment_out, sems.at[1]),
    ]
    for copy in copies:
        copy.start()
    copies[0].wait()
    low_ref[...] = master_out[...].astype(bf16)
    copies[1].wait()


def load_body(second_ref, _, second_out, sems):
    copy = pltpu.make_async_copy(second_ref, second_out, sems.at[0])
    copy.start()
    copy.wait()


def spread_body(count, micro, scale, plan_ref, *refs):
    cots, (low_ref, ordered_ref), outs = refs[:count], refs[count : count + 2], refs[count + 2 :]
    rows = cots[0].shape[0]
    size = rows // micro
    for k in range(count):
        for i in range(micro):
            at = pl.multiple_of(plan_ref[i] * size, size)
            ordered_ref[k * rows + i * size : k * rows + (i + 1) * size, :] = cots[k][
                pl.ds(at, size), :
            ]
    step = 256
    for at in range(0, low_ref.shape[0], step):
        product = lax.dot_general(
            ordered_ref[...],
            low_ref[at : at + step, :],
            (((1,), (1,)), ((), ())),
            preferred_element_type=f32,
        )
        for k in range(count):
            outs[k][:, at : at + step] = (product[k * rows : (k + 1) * rows, :] * scale).astype(bf16)


def grad_body(count, head, scale, place_ref, owner_ref, *refs):
    normed, refs = refs[:count], refs[count:]
    ordered_ref, master_ref, moment_ref, second_ref, moment_out, second_out = refs[:6]
    outs, mark_ref, joined, fresh = refs[6 : 6 + count], *refs[6 + count :]
    tok_count = normed[0].shape[1]
    kv_cols = master_ref.shape[1]
    mark_ref[...] = jnp.zeros_like(mark_ref)
    for k in range(count):
        joined[:, k * tok_count : (k + 1) * tok_count] = normed[k][...]
    step = 256
    size = joined.shape[0]
    rows = pl.ds(pl.multiple_of(pl.program_id(0) * size, size), size)
    for at in range(0, kv_cols, step):
        here = slice(at, at + step)
        part = jnp.dot(joined[...], ordered_ref[:, here], preferred_element_type=f32)
        moment_new = beta_one * moment_ref[rows, here] + ((1.0 - beta_one) * scale) * part
        second_new = beta_two * second_ref[rows, here] + (
            ((1.0 - beta_two) * scale * scale) * part
        ) * part
        moment_out[:, here] = moment_new
        second_out[:, here] = second_new
        scaled = second_new * (1.0 / bias_two)
        root = scaled * lax.rsqrt(scaled) + adam_eps
        weights = master_ref[rows, here] * (1.0 - learn_rate * weight_decay) - (
            moment_new * (learn_rate / bias_one)
        ) * pl.reciprocal(root, approx=True)
        fresh[:, here] = weights.astype(bf16)
    for k in range(count):
        owner = owner_ref[place_ref[0] ^ k] * head
        for p in range(2):
            lanes = pl.ds(pl.multiple_of(p * (kv_cols // 2) + owner, head), head)
            outs[k][p * head : (p + 1) * head, :] = fresh[:, lanes].T


def own_body(count, place_ref, core_ref, tok_ref, gain_ref, inv_ref, *refs):
    spread, (_, keep_ref, give_ref) = refs[:count], refs[count:]
    place = place_ref[0]
    core = core_ref[0]
    width = tok_ref.shape[1]
    cols = width // count
    half = tok_ref.shape[0] // 2
    for out_ref, pick in ((give_ref, 1 - core), (keep_ref, core)):
        rows = pl.ds(pl.multiple_of(pick * half, half), half)
        inverse = inv_ref[rows, :]
        total = jnp.zeros((half, 1), f32)
        for k in range(count):
            part = part_of(place, k, cols)
            scaled = spread[k][rows, :].astype(f32) * gain_ref[:, part]
            total = total + jnp.sum(
                scaled * tok_ref[rows, part].astype(f32), axis=-1, keepdims=True
            )
        factor = inverse * inverse * inverse * (total / width)
        for k in range(count):
            part = part_of(place, k, cols)
            scaled = spread[k][rows, :].astype(f32) * gain_ref[:, part]
            out_ref[:, part] = (
                inverse * scaled - tok_ref[rows, part].astype(f32) * factor
            ).astype(bf16)


def pair_body(chip_ref, keep_ref, got_ref, one_ref, two_ref):
    z = chip_ref[0]
    half = one_ref.shape[0]
    for out_ref, top in ((one_ref, z == 3), (two_ref, z == 2)):
        rows = pl.ds(pl.multiple_of(jnp.where(top, 0, half), half), half)
        out_ref[...] = (keep_ref[rows, :].astype(f32) + got_ref[rows, :].astype(f32)).astype(bf16)


def middle_body(chip_ref, keep_ref, got_ref, one_ref, two_ref, three_ref, four_ref):
    z = chip_ref[0]
    half = one_ref.shape[0]
    rows = pl.ds(pl.multiple_of(jnp.where(z == 2, half, 0), half), half)
    one = one_ref[...].astype(f32)
    two = two_ref[...].astype(f32)
    mine = keep_ref[rows, :].astype(f32) + got_ref[rows, :].astype(f32) + two
    three_ref[...] = (mine + jnp.where(z == 1, one, 0.0)).astype(bf16)
    four_ref[...] = (mine + one).astype(bf16)


def last_body(chip_ref, core_ref, keep_ref, got_ref, one_ref, two_ref, three_ref, four_ref, _, out_ref, send_ref):
    z = chip_ref[0]
    core = core_ref[0]
    half = one_ref.shape[0]
    for part in range(2):
        rows = slice(part * half, (part + 1) * half)
        one = one_ref[...].astype(f32)
        two = two_ref[...].astype(f32)
        three = three_ref[...].astype(f32)
        if part == 0:
            above = jnp.where(z == 1, one + two, three)
        else:
            four = four_ref[...].astype(f32)
            above = jnp.where(z == 0, four, jnp.where(z == 1, three, two))
        keep = keep_ref[rows, :].astype(f32)
        got = got_ref[rows, :].astype(f32)
        both = keep + got + above
        out_ref[rows, :] = jnp.where(core == 0, both, keep + above).astype(bf16)
        send_ref[rows, :] = jnp.where(core == 0, got + above, both).astype(bf16)


def place_body(place_ref, part_ref, *refs):
    refs[-1][...] = part_ref[...]


def marked_body(place_ref, part_ref, _, out_ref, mark_ref):
    out_ref[...] = part_ref[...]
    mark_ref[...] = jnp.zeros_like(mark_ref)


def shards(tokens, cotangents, norm_gain, master, moment, second, head_owner, plan):
    tok_rows, cot_rows = tokens[0], cotangents[0]
    master_rows, moment_rows, second_rows = master[0], moment[0], second[0]
    tok_count, width = tok_rows.shape
    kv_cols = cot_rows.shape[1]
    heads = head_owner.shape[1]
    head = kv_cols // (2 * heads)
    scale = width ** (-0.5)
    count = lax.axis_size("fsdp")
    place = lax.axis_index("fsdp").astype(jnp.int32)[None]
    section = lax.axis_index("section").astype(jnp.int32)
    core, chip = (section & 1)[None], (section >> 1)[None]
    cols = width // count
    half = tok_count // 2
    sds = jax.ShapeDtypeStruct
    dests = range(1, count)
    anywhere = pl.BlockSpec(memory_space=pl.ANY)
    mark = sds((8, 128), f32)

    cots = [cot_rows] + [swap(cot_rows, "fsdp", k) for k in dests]

    inverse, *normed = call(
        "prep",
        functools.partial(prep_body, count),
        (1,),
        1,
        [whole((tok_count, width)), whole((1, width))],
        [whole((tok_count, 1))] + [whole((cols, tok_count))] * count,
        [sds((tok_count, 1), f32)] + [sds((cols, tok_count), bf16)] * count,
    )(place, tok_rows, norm_gain)
    normed = [normed[0]] + [swap(normed[k], "fsdp", k) for k in dests]

    rows_step = 256
    resident = pl.BlockSpec(memory_space=pltpu.VMEM)
    distant = pl.BlockSpec(memory_space=pltpu.HBM)
    wide = sds((cols, kv_cols), f32)
    master_near, moment_near, low = call(
        "low",
        low_body,
        (),
        0,
        [distant, distant, anywhere],
        [resident] * 3,
        [wide, wide, sds((cols, kv_cols), bf16)],
        scratch=[pltpu.SemaphoreType.DMA((2,))],
    )(master_rows, moment_rows, inverse)
    ordered, *spread = call(
        "spread",
        functools.partial(spread_body, count, plan.shape[0], scale),
        (),
        1,
        [resident] * (count + 1),
        [resident] * (count + 1),
        [sds((count * tok_count, kv_cols), bf16)] + [sds((tok_count, cols), bf16)] * count,
        work=10**10,
    )(plan, *cots, low)
    (second_near,) = call(
        "load",
        load_body,
        (),
        0,
        [distant, anywhere],
        [resident],
        [wide],
        scratch=[pltpu.SemaphoreType.DMA((1,))],
    )(second_rows, spread[0])
    spread = [spread[0]] + [swap(spread[k], "fsdp", k) for k in dests]

    state = pl.BlockSpec((rows_step, kv_cols), lambda i, *_: (i, 0))
    moment_new, second_new, *rollout_parts, grad_mark = call(
        "grad",
        functools.partial(grad_body, count, head, scale),
        (cols // rows_step,),
        2,
        [pl.BlockSpec((rows_step, tok_count), lambda i, *_: (i, 0))] * count
        + [resident, resident, resident, resident],
        [state, state]
        + [pl.BlockSpec((2 * head, rows_step), lambda i, *_: (0, i))] * count
        + [whole((8, 128))],
        [sds((cols, kv_cols), f32)] * 2 + [sds((2 * head, cols), bf16)] * count + [mark],
        scratch=[
            pltpu.VMEM((rows_step, count * tok_count), bf16),
            pltpu.VMEM((rows_step, kv_cols), bf16),
        ],
        vmem=20,
    )(place, head_owner[0], *normed, ordered, master_near, moment_near, second_near)

    rollout = ()
    rollout_mark = ()
    for k in (0, 3, 1, 2):
        part = swap(rollout_parts[k], "fsdp", k) if k else rollout_parts[k]
        final = k == 2
        rollout, *rollout_mark = call(
            "place",
            marked_body if final else place_body,
            (1,),
            1,
            [whole((2 * head, cols))] + ([anywhere] if k else []),
            [pl.BlockSpec((2 * head, cols), lambda i, place_ref, k=k: (0, place_ref[0] ^ k))]
            + ([whole((8, 128))] if final else []),
            [sds((2 * head, width), bf16)] + ([mark] if final else []),
            aliases={2: 0} if k else None,
            work=10**9,
        )(place, part, *([rollout] if k else []))

    keep, give = call(
        "own",
        functools.partial(own_body, count),
        (1,),
        2,
        [whole((tok_count, width)), whole((1, width)), whole((tok_count, 1))]
        + [whole((tok_count, cols))] * count
        + [anywhere],
        [whole((half, width))] * 2,
        [sds((half, width), bf16)] * 2,
    )(place, core, tok_rows, norm_gain, inverse, *spread, grad_mark)
    got = swap(give, "section", 1)

    def chips(pairs):
        return [(2 * a + c, 2 * b + c) for c in range(2) for a, b in pairs]

    quarter = half // 2
    full, part = whole((half, width)), whole((quarter, width))
    piece = sds((quarter, width), bf16)
    one, two = call("pair", pair_body, (1,), 1, [full, full], [part, part], [piece, piece])(
        chip, keep, got
    )
    one = lax.ppermute(one, "section", chips([(3, 1), (1, 2)]))
    two = lax.ppermute(two, "section", chips([(2, 1), (3, 2)]))
    three, four = call(
        "middle", middle_body, (1,), 1, [full, full, part, part], [part, part], [piece, piece]
    )(chip, keep, got, one, two)
    three = lax.ppermute(three, "section", chips([(1, 0), (2, 1), (3, 2)]))
    four = lax.ppermute(four, "section", chips([(2, 0)]))
    grads, send = call(
        "last",
        last_body,
        (1,),
        2,
        [full, full, part, part, part, part, anywhere],
        [pl.BlockSpec((half, width), lambda i, chip_ref, core_ref: (core_ref[0], 0)), full],
        [sds((tok_count, width), bf16), sds((half, width), bf16)],
    )(chip, core, keep, got, one, two, three, four, *rollout_mark)
    other = swap(send, "section", 1)
    grads = call(
        "join",
        place_body,
        (1,),
        1,
        [full, anywhere],
        pl.BlockSpec((half, width), lambda i, core_ref: (1 - core_ref[0], 0)),
        sds((tok_count, width), bf16),
        aliases={2: 0},
    )(core, other, grads)
    return (grads[None], moment_new[None], second_new[None], rollout[None])


def choose(*args):
    tokens, cotangents, norm_gain, master, moment, second, head_owner, plan = args
    count, sections = lax.axis_size("fsdp"), lax.axis_size("section")
    tok_count, width = tokens.shape[1:]
    kv_cols, heads = cotangents.shape[2], head_owner.shape[1]
    fits = (
        count == 4
        and sections == 8
        and heads == count
        and plan.shape[0] == 4
        and kv_cols == 2 * heads * 128
        and (width // count) % 256 == 0
        and tok_count % 128 == 0
        and tok_count % (16 * plan.shape[0]) == 0
    )
    return (shards if fits else shards_any)(*args)


def solution(mesh):
    in_specs = (
        P("section", "fsdp", None),
        P("section", "fsdp", None),
        P("section", None),
        P("section", "fsdp", None),
        P("section", "fsdp", None),
        P("section", "fsdp", None),
        P("section", None),
        P(),
    )
    out_specs = (
        P("section", "fsdp", None),
        P("section", "fsdp", None),
        P("section", "fsdp", None),
        P("section", "fsdp", None),
    )
    return jax.shard_map(choose, mesh=mesh, in_specs=in_specs, out_specs=out_specs, check_vma=False)
```

```python
import functools

import jax
import jax.numpy as jnp
from jax import lax
from jax.experimental import pallas as pl
from jax.experimental.pallas import tpu as pltpu
from jax.sharding import PartitionSpec as P

beta_one = 0.9
beta_two = 0.95
bias_one = 1.0 - 0.9**10
bias_two = 1.0 - 0.95**10
adam_eps = 1e-08
learn_rate = 0.02
weight_decay = 0.1
norm_eps = 1e-06

bf16 = jnp.bfloat16
f32 = jnp.float32


def swap(x, axis, k):
    count = lax.axis_size(axis)
    return lax.ppermute(x, axis, [(i, i ^ k) for i in range(count)])


def adam_step(master, moment, second, gradient):
    moment_new = beta_one * moment + (1.0 - beta_one) * gradient
    second_new = beta_two * second + (1.0 - beta_two) * gradient * gradient
    update = moment_new / bias_one / (jnp.sqrt(second_new / bias_two) + adam_eps)
    weights = master - learn_rate * (update + weight_decay * master)
    return (moment_new, second_new, weights)


def plan_rows(cot_rows, plan):
    micro_count = plan.shape[0]
    blocks = cot_rows.reshape(micro_count, -1, cot_rows.shape[-1])
    return jnp.take(blocks, plan, axis=0).reshape(cot_rows.shape)


def suffix_sum(own_term, axis):
    count = lax.axis_size(axis)
    place = lax.axis_index(axis)
    low = own_term.astype(bf16)
    pair = lax.ppermute(low, axis, [(i + 1, i) for i in range(0, count, 2)])
    total = own_term + pair.astype(f32)
    above = jnp.zeros_like(low)
    for z in range(count // 2 - 1, 0, -1):
        got = lax.ppermute(total.astype(bf16), axis, [(2 * z, 2 * z - 2)])
        total = total + got.astype(f32)
        above = above + got
    from_pair = lax.ppermute(above, axis, [(i, i + 1) for i in range(0, count, 2)])
    return jnp.where(place % 2 == 0, total, own_term + from_pair.astype(f32))


def shards_any(tokens, cotangents, norm_gain, master, moment, second, head_owner, plan):
    tok_rows = tokens[0]
    gain_row = norm_gain[0]
    master_rows = master[0]
    owner_row = head_owner[0]
    width = tok_rows.shape[1]
    tok_count = tok_rows.shape[0]
    proj_scale = width ** (-0.5)
    count = lax.axis_size("fsdp")
    place = lax.axis_index("fsdp")
    cols = width // count

    def block_of(x, k):
        return lax.dynamic_slice_in_dim(x, (place ^ k) * cols, cols, axis=-1)

    ordered = plan_rows(cotangents[0], plan)
    all_ordered = [ordered] + [swap(ordered, "fsdp", k) for k in range(1, count)]
    widened = tok_rows.astype(f32)
    inverse = lax.rsqrt(jnp.mean(widened * widened, axis=-1, keepdims=True) + norm_eps)
    normed = (widened * inverse * gain_row).astype(bf16)
    all_normed = [block_of(normed, 0)] + [
        swap(block_of(normed, k), "fsdp", k) for k in range(1, count)
    ]
    low_weights = master_rows.astype(bf16)
    spread = []
    for k in range(count):
        part = (
            jnp.einsum("tc,rc->tr", all_ordered[k], low_weights, preferred_element_type=f32)
            * proj_scale
        )
        spread.append(part if k == 0 else swap(part.astype(bf16), "fsdp", k).astype(f32))

    gradient = (
        jnp.einsum(
            "td,tc->dc",
            jnp.concatenate(all_normed, axis=0),
            jnp.concatenate(all_ordered, axis=0),
            preferred_element_type=f32,
        )
        * proj_scale
    )
    moment_new, second_new, weights = adam_step(master_rows, moment[0], second[0], gradient)
    heads = owner_row.shape[0]
    low_new = weights.astype(bf16).reshape(cols, 2, heads, -1)
    arranged = jnp.take(low_new, owner_row, axis=2).transpose(2, 1, 3, 0).reshape(count, -1, cols)
    rollout = jnp.zeros((arranged.shape[1], width), bf16)
    for k in range(count):
        part = lax.dynamic_index_in_dim(arranged, place ^ k, 0, False)
        if k:
            part = swap(part, "fsdp", k)
        rollout = lax.dynamic_update_slice_in_dim(rollout, part, (place ^ k) * cols, axis=1)

    tok_k = [block_of(tok_rows, k).astype(f32) for k in range(count)]
    scaled = [spread[k] * block_of(gain_row, k) for k in range(count)]
    mean_term = sum(jnp.sum(scaled[k] * tok_k[k], axis=-1, keepdims=True) for k in range(count)) / width
    factor = inverse * inverse * inverse * mean_term
    own_term = jnp.concatenate(
        [inverse * scaled[k] - tok_k[k] * factor for k in range(count)], axis=0
    )
    summed = suffix_sum(own_term, "section").astype(bf16).reshape(count, tok_count, cols)
    input_grads = jnp.zeros((tok_count, width), bf16)
    for k in range(count):
        input_grads = lax.dynamic_update_slice_in_dim(
            input_grads, summed[k], (place ^ k) * cols, axis=1
        )
    return (input_grads[None], moment_new[None], second_new[None], rollout[None])


def call(name, body, grid, prefetch, in_specs, out_specs, out_shape, scratch=(), aliases=None, vmem=16, work=1):
    return pl.pallas_call(
        body,
        grid_spec=pltpu.PrefetchScalarGridSpec(
            num_scalar_prefetch=prefetch,
            grid=grid,
            in_specs=in_specs,
            out_specs=out_specs,
            scratch_shapes=list(scratch),
        ),
        out_shape=out_shape,
        input_output_aliases=aliases or {},
        name=name,
        compiler_params=pltpu.CompilerParams(
            vmem_limit_bytes=vmem * 1024 * 1024,
            dimension_semantics=("arbitrary",) * len(grid),
        ),
        cost_estimate=pl.CostEstimate(flops=work, bytes_accessed=1, transcendentals=0),
    )


def whole(shape):
    return pl.BlockSpec(shape, lambda *_: (0,) * len(shape))


def part_of(place, k, cols):
    return pl.ds(pl.multiple_of((place ^ k) * cols, 128), cols)


def prep_body(count, place_ref, core_ref, chip_ref, tok_ref, gain_ref, inv_ref, *out_refs):
    place = place_ref[0]
    width = tok_ref.shape[1]
    cols = width // count
    total = jnp.zeros((tok_ref.shape[0], 1), f32)
    for k in range(count):
        x = tok_ref[:, k * cols : (k + 1) * cols].astype(f32)
        total = total + jnp.sum(x * x, axis=-1, keepdims=True)
    inverse = lax.rsqrt(total / width + norm_eps)
    inv_ref[...] = inverse
    for k in range(count):
        part = part_of(place, k, cols)
        x = tok_ref[:, part].astype(f32)
        out_refs[k][...] = (x * inverse * gain_ref[:, part]).astype(bf16).T


def low_body(master_ref, _, low_ref):
    low_ref[...] = master_ref[...].astype(bf16)


def spread_body(count, micro, scale, plan_ref, *refs):
    cots, (low_ref, ordered_ref), outs = refs[:count], refs[count : count + 2], refs[count + 2 :]
    rows = cots[0].shape[0]
    size = rows // micro
    for k in range(count):
        for i in range(micro):
            at = pl.multiple_of(plan_ref[i] * size, size)
            ordered_ref[k * rows + i * size : k * rows + (i + 1) * size, :] = cots[k][
                pl.ds(at, size), :
            ]
    step = 256
    for at in range(0, low_ref.shape[0], step):
        product = lax.dot_general(
            ordered_ref[...],
            low_ref[at : at + step, :],
            (((1,), (1,)), ((), ())),
            preferred_element_type=f32,
        )
        for k in range(count):
            outs[k][:, at : at + step] = (product[k * rows : (k + 1) * rows, :] * scale).astype(bf16)


def grad_body(count, head, scale, place_ref, owner_ref, *refs):
    normed, refs = refs[:count], refs[count:]
    ordered_ref, master_ref, moment_ref, second_ref, moment_out, second_out = refs[:6]
    outs, mark_ref, joined, fresh = refs[6 : 6 + count], *refs[6 + count :]
    tok_count = normed[0].shape[1]
    kv_cols = master_ref.shape[1]
    mark_ref[...] = jnp.zeros_like(mark_ref)
    for k in range(count):
        joined[:, k * tok_count : (k + 1) * tok_count] = normed[k][...]
    step = 256
    size = joined.shape[0]
    rows = pl.ds(pl.multiple_of(pl.program_id(0) * size, size), size)
    for at in range(0, kv_cols, step):
        here = slice(at, at + step)
        part = jnp.dot(joined[...], ordered_ref[:, here], preferred_element_type=f32)
        moment_new = beta_one * moment_ref[rows, here] + ((1.0 - beta_one) * scale) * part
        second_new = beta_two * second_ref[rows, here] + (
            ((1.0 - beta_two) * scale * scale) * part
        ) * part
        moment_out[:, here] = moment_new
        second_out[:, here] = second_new
        scaled = second_new * (1.0 / bias_two)
        root = scaled * lax.rsqrt(scaled) + adam_eps
        weights = master_ref[rows, here] * (1.0 - learn_rate * weight_decay) - (
            moment_new * (learn_rate / bias_one)
        ) * pl.reciprocal(root, approx=True)
        fresh[:, here] = weights.astype(bf16)
    for k in range(count):
        owner = owner_ref[place_ref[0] ^ k] * head
        for p in range(2):
            lanes = pl.ds(pl.multiple_of(p * (kv_cols // 2) + owner, head), head)
            outs[k][p * head : (p + 1) * head, :] = fresh[:, lanes].T


def own_body(count, place_ref, core_ref, tok_ref, gain_ref, inv_ref, *refs):
    spread, (_, keep_ref, give_ref) = refs[:count], refs[count:]
    place = place_ref[0]
    core = core_ref[0]
    width = tok_ref.shape[1]
    cols = width // count
    half = tok_ref.shape[0] // 2
    for out_ref, pick in ((give_ref, 1 - core), (keep_ref, core)):
        rows = pl.ds(pl.multiple_of(pick * half, half), half)
        inverse = inv_ref[rows, :]
        total = jnp.zeros((half, 1), f32)
        for k in range(count):
            part = part_of(place, k, cols)
            scaled = spread[k][rows, :].astype(f32) * gain_ref[:, part]
            total = total + jnp.sum(
                scaled * tok_ref[rows, part].astype(f32), axis=-1, keepdims=True
            )
        factor = inverse * inverse * inverse * (total / width)
        for k in range(count):
            part = part_of(place, k, cols)
            scaled = spread[k][rows, :].astype(f32) * gain_ref[:, part]
            out_ref[:, part] = (
                inverse * scaled - tok_ref[rows, part].astype(f32) * factor
            ).astype(bf16)


def pair_body(chip_ref, keep_ref, got_ref, one_ref, two_ref):
    z = chip_ref[0]
    half = one_ref.shape[0]
    for out_ref, top in ((one_ref, z == 3), (two_ref, z == 2)):
        rows = pl.ds(pl.multiple_of(jnp.where(top, 0, half), half), half)
        out_ref[...] = (keep_ref[rows, :].astype(f32) + got_ref[rows, :].astype(f32)).astype(bf16)


def middle_body(chip_ref, keep_ref, got_ref, one_ref, two_ref, three_ref, four_ref):
    z = chip_ref[0]
    half = one_ref.shape[0]
    rows = pl.ds(pl.multiple_of(jnp.where(z == 2, half, 0), half), half)
    one = one_ref[...].astype(f32)
    two = two_ref[...].astype(f32)
    mine = keep_ref[rows, :].astype(f32) + got_ref[rows, :].astype(f32) + two
    three_ref[...] = (mine + jnp.where(z == 1, one, 0.0)).astype(bf16)
    four_ref[...] = (mine + one).astype(bf16)


def last_body(chip_ref, core_ref, keep_ref, got_ref, one_ref, two_ref, three_ref, four_ref, _, out_ref, send_ref):
    z = chip_ref[0]
    core = core_ref[0]
    half = one_ref.shape[0]
    for part in range(2):
        rows = slice(part * half, (part + 1) * half)
        one = one_ref[...].astype(f32)
        two = two_ref[...].astype(f32)
        three = three_ref[...].astype(f32)
        if part == 0:
            above = jnp.where(z == 1, one + two, three)
        else:
            four = four_ref[...].astype(f32)
            above = jnp.where(z == 0, four, jnp.where(z == 1, three, two))
        keep = keep_ref[rows, :].astype(f32)
        got = got_ref[rows, :].astype(f32)
        both = keep + got + above
        out_ref[rows, :] = jnp.where(core == 0, both, keep + above).astype(bf16)
        send_ref[rows, :] = jnp.where(core == 0, got + above, both).astype(bf16)


def place_body(place_ref, part_ref, *refs):
    refs[-1][...] = part_ref[...]


def marked_body(place_ref, part_ref, _, out_ref, mark_ref):
    out_ref[...] = part_ref[...]
    mark_ref[...] = jnp.zeros_like(mark_ref)


def shards(tokens, cotangents, norm_gain, master, moment, second, head_owner, plan):
    tok_rows, cot_rows = tokens[0], cotangents[0]
    master_rows, moment_rows, second_rows = master[0], moment[0], second[0]
    tok_count, width = tok_rows.shape
    kv_cols = cot_rows.shape[1]
    heads = head_owner.shape[1]
    head = kv_cols // (2 * heads)
    scale = width ** (-0.5)
    count = lax.axis_size("fsdp")
    place = lax.axis_index("fsdp").astype(jnp.int32)[None]
    section = lax.axis_index("section").astype(jnp.int32)
    core, chip = (section & 1)[None], (section >> 1)[None]
    cols = width // count
    half = tok_count // 2
    sds = jax.ShapeDtypeStruct
    dests = range(1, count)
    anywhere = pl.BlockSpec(memory_space=pl.ANY)
    resident = pl.BlockSpec(memory_space=pltpu.VMEM)
    mark = sds((8, 128), f32)

    cots = [cot_rows] + [swap(cot_rows, "fsdp", k) for k in dests]

    inverse, *normed = call(
        "prep",
        functools.partial(prep_body, count),
        (1,),
        3,
        [whole((tok_count, width)), whole((1, width))],
        [whole((tok_count, 1))] + [whole((cols, tok_count))] * count,
        [sds((tok_count, 1), f32)] + [sds((cols, tok_count), bf16)] * count,
    )(place, core, chip, tok_rows, norm_gain)
    normed = [normed[0]] + [swap(normed[k], "fsdp", k) for k in dests]

    rows_step = 256
    low = call(
        "low",
        low_body,
        (cols // rows_step,),
        0,
        [pl.BlockSpec((rows_step, kv_cols), lambda i: (i, 0)), anywhere],
        pl.BlockSpec((rows_step, kv_cols), lambda i: (i, 0)),
        sds((cols, kv_cols), bf16),
    )(master_rows, inverse)
    ordered, *spread = call(
        "spread",
        functools.partial(spread_body, count, plan.shape[0], scale),
        (),
        1,
        [resident] * (count + 1),
        [resident] * (count + 1),
        [sds((count * tok_count, kv_cols), bf16)] + [sds((tok_count, cols), bf16)] * count,
        work=10**10,
    )(plan, *cots, low)
    spread = [spread[0]] + [swap(spread[k], "fsdp", k) for k in dests]

    state = pl.BlockSpec((rows_step, kv_cols), lambda i, *_: (i, 0))
    moment_new, second_new, *rollout_parts, grad_mark = call(
        "grad",
        functools.partial(grad_body, count, head, scale),
        (cols // rows_step,),
        2,
        [pl.BlockSpec((rows_step, tok_count), lambda i, *_: (i, 0))] * count
        + [resident, resident, resident, resident],
        [state, state]
        + [pl.BlockSpec((2 * head, rows_step), lambda i, *_: (0, i))] * count
        + [whole((8, 128))],
        [sds((cols, kv_cols), f32)] * 2 + [sds((2 * head, cols), bf16)] * count + [mark],
        scratch=[
            pltpu.VMEM((rows_step, count * tok_count), bf16),
            pltpu.VMEM((rows_step, kv_cols), bf16),
        ],
        vmem=20,
    )(place, head_owner[0], *normed, ordered, master_rows, moment_rows, second_rows)

    rollout = ()
    rollout_mark = ()
    for k in (0, 3, 1, 2):
        part = swap(rollout_parts[k], "fsdp", k) if k else rollout_parts[k]
        final = k == 2
        rollout, *rollout_mark = call(
            "place",
            marked_body if final else place_body,
            (1,),
            1,
            [whole((2 * head, cols))] + ([anywhere] if k else []),
            [pl.BlockSpec((2 * head, cols), lambda i, place_ref, k=k: (0, place_ref[0] ^ k))]
            + ([whole((8, 128))] if final else []),
            [sds((2 * head, width), bf16)] + ([mark] if final else []),
            aliases={2: 0} if k else None,
            work=10**9,
        )(place, part, *([rollout] if k else []))

    keep, give = call(
        "own",
        functools.partial(own_body, count),
        (1,),
        2,
        [whole((tok_count, width)), whole((1, width)), whole((tok_count, 1))]
        + [whole((tok_count, cols))] * count
        + [anywhere],
        [whole((half, width))] * 2,
        [sds((half, width), bf16)] * 2,
    )(place, core, tok_rows, norm_gain, inverse, *spread, grad_mark)
    got = swap(give, "section", 1)

    def chips(pairs):
        return [(2 * a + c, 2 * b + c) for c in range(2) for a, b in pairs]

    quarter = half // 2
    full, part = whole((half, width)), whole((quarter, width))
    piece = sds((quarter, width), bf16)
    one, two = call("pair", pair_body, (1,), 1, [full, full], [part, part], [piece, piece])(
        chip, keep, got
    )
    one = lax.ppermute(one, "section", chips([(3, 1), (1, 2)]))
    two = lax.ppermute(two, "section", chips([(2, 1), (3, 2)]))
    three, four = call(
        "middle", middle_body, (1,), 1, [full, full, part, part], [part, part], [piece, piece]
    )(chip, keep, got, one, two)
    three = lax.ppermute(three, "section", chips([(1, 0), (2, 1), (3, 2)]))
    four = lax.ppermute(four, "section", chips([(2, 0)]))
    grads, send = call(
        "last",
        last_body,
        (1,),
        2,
        [full, full, part, part, part, part, anywhere],
        [pl.BlockSpec((half, width), lambda i, chip_ref, core_ref: (core_ref[0], 0)), full],
        [sds((tok_count, width), bf16), sds((half, width), bf16)],
    )(chip, core, keep, got, one, two, three, four, *rollout_mark)
    other = swap(send, "section", 1)
    grads = call(
        "join",
        place_body,
        (1,),
        1,
        [full, anywhere],
        pl.BlockSpec((half, width), lambda i, core_ref: (1 - core_ref[0], 0)),
        sds((tok_count, width), bf16),
        aliases={2: 0},
    )(core, other, grads)
    return (grads[None], moment_new[None], second_new[None], rollout[None])


def choose(*args):
    tokens, cotangents, norm_gain, master, moment, second, head_owner, plan = args
    count, sections = lax.axis_size("fsdp"), lax.axis_size("section")
    tok_count, width = tokens.shape[1:]
    kv_cols, heads = cotangents.shape[2], head_owner.shape[1]
    fits = (
        count == 4
        and sections == 8
        and heads == count
        and plan.shape[0] == 4
        and kv_cols == 2 * heads * 128
        and (width // count) % 256 == 0
        and tok_count % 128 == 0
        and tok_count % (16 * plan.shape[0]) == 0
    )
    return (shards if fits else shards_any)(*args)


def solution(mesh):
    in_specs = (
        P("section", "fsdp", None),
        P("section", "fsdp", None),
        P("section", None),
        P("section", "fsdp", None),
        P("section", "fsdp", None),
        P("section", "fsdp", None),
        P("section", None),
        P(),
    )
    out_specs = (
        P("section", "fsdp", None),
        P("section", "fsdp", None),
        P("section", "fsdp", None),
        P("section", "fsdp", None),
    )
    return jax.shard_map(choose, mesh=mesh, in_specs=in_specs, out_specs=out_specs, check_vma=False)
```

```python
import functools

import jax
import jax.numpy as jnp
from jax import lax
from jax.experimental import pallas as pl
from jax.experimental.pallas import tpu as pltpu
from jax.sharding import PartitionSpec as P

beta_one = 0.9
beta_two = 0.95
bias_one = 1.0 - 0.9**10
bias_two = 1.0 - 0.95**10
adam_eps = 1e-08
learn_rate = 0.02
weight_decay = 0.1
norm_eps = 1e-06

bf16 = jnp.bfloat16
f32 = jnp.float32


def swap(x, axis, k):
    count = lax.axis_size(axis)
    return lax.ppermute(x, axis, [(i, i ^ k) for i in range(count)])


def adam_step(master, moment, second, gradient):
    moment_new = beta_one * moment + (1.0 - beta_one) * gradient
    second_new = beta_two * second + (1.0 - beta_two) * gradient * gradient
    update = moment_new / bias_one / (jnp.sqrt(second_new / bias_two) + adam_eps)
    weights = master - learn_rate * (update + weight_decay * master)
    return (moment_new, second_new, weights)


def plan_rows(cot_rows, plan):
    micro_count = plan.shape[0]
    blocks = cot_rows.reshape(micro_count, -1, cot_rows.shape[-1])
    return jnp.take(blocks, plan, axis=0).reshape(cot_rows.shape)


def suffix_sum(own_term, axis):
    count = lax.axis_size(axis)
    place = lax.axis_index(axis)
    low = own_term.astype(bf16)
    pair = lax.ppermute(low, axis, [(i + 1, i) for i in range(0, count, 2)])
    total = own_term + pair.astype(f32)
    above = jnp.zeros_like(low)
    for z in range(count // 2 - 1, 0, -1):
        got = lax.ppermute(total.astype(bf16), axis, [(2 * z, 2 * z - 2)])
        total = total + got.astype(f32)
        above = above + got
    from_pair = lax.ppermute(above, axis, [(i, i + 1) for i in range(0, count, 2)])
    return jnp.where(place % 2 == 0, total, own_term + from_pair.astype(f32))


def shards_any(tokens, cotangents, norm_gain, master, moment, second, head_owner, plan):
    tok_rows = tokens[0]
    gain_row = norm_gain[0]
    master_rows = master[0]
    owner_row = head_owner[0]
    width = tok_rows.shape[1]
    tok_count = tok_rows.shape[0]
    proj_scale = width ** (-0.5)
    count = lax.axis_size("fsdp")
    place = lax.axis_index("fsdp")
    cols = width // count

    def block_of(x, k):
        return lax.dynamic_slice_in_dim(x, (place ^ k) * cols, cols, axis=-1)

    ordered = plan_rows(cotangents[0], plan)
    all_ordered = [ordered] + [swap(ordered, "fsdp", k) for k in range(1, count)]
    widened = tok_rows.astype(f32)
    inverse = lax.rsqrt(jnp.mean(widened * widened, axis=-1, keepdims=True) + norm_eps)
    normed = (widened * inverse * gain_row).astype(bf16)
    all_normed = [block_of(normed, 0)] + [
        swap(block_of(normed, k), "fsdp", k) for k in range(1, count)
    ]
    low_weights = master_rows.astype(bf16)
    spread = []
    for k in range(count):
        part = (
            jnp.einsum("tc,rc->tr", all_ordered[k], low_weights, preferred_element_type=f32)
            * proj_scale
        )
        spread.append(part if k == 0 else swap(part.astype(bf16), "fsdp", k).astype(f32))

    gradient = (
        jnp.einsum(
            "td,tc->dc",
            jnp.concatenate(all_normed, axis=0),
            jnp.concatenate(all_ordered, axis=0),
            preferred_element_type=f32,
        )
        * proj_scale
    )
    moment_new, second_new, weights = adam_step(master_rows, moment[0], second[0], gradient)
    heads = owner_row.shape[0]
    low_new = weights.astype(bf16).reshape(cols, 2, heads, -1)
    arranged = jnp.take(low_new, owner_row, axis=2).transpose(2, 1, 3, 0).reshape(count, -1, cols)
    rollout = jnp.zeros((arranged.shape[1], width), bf16)
    for k in range(count):
        part = lax.dynamic_index_in_dim(arranged, place ^ k, 0, False)
        if k:
            part = swap(part, "fsdp", k)
        rollout = lax.dynamic_update_slice_in_dim(rollout, part, (place ^ k) * cols, axis=1)

    tok_k = [block_of(tok_rows, k).astype(f32) for k in range(count)]
    scaled = [spread[k] * block_of(gain_row, k) for k in range(count)]
    mean_term = sum(jnp.sum(scaled[k] * tok_k[k], axis=-1, keepdims=True) for k in range(count)) / width
    factor = inverse * inverse * inverse * mean_term
    own_term = jnp.concatenate(
        [inverse * scaled[k] - tok_k[k] * factor for k in range(count)], axis=0
    )
    summed = suffix_sum(own_term, "section").astype(bf16).reshape(count, tok_count, cols)
    input_grads = jnp.zeros((tok_count, width), bf16)
    for k in range(count):
        input_grads = lax.dynamic_update_slice_in_dim(
            input_grads, summed[k], (place ^ k) * cols, axis=1
        )
    return (input_grads[None], moment_new[None], second_new[None], rollout[None])


def call(name, body, grid, prefetch, in_specs, out_specs, out_shape, scratch=(), aliases=None, vmem=16, work=1):
    return pl.pallas_call(
        body,
        grid_spec=pltpu.PrefetchScalarGridSpec(
            num_scalar_prefetch=prefetch,
            grid=grid,
            in_specs=in_specs,
            out_specs=out_specs,
            scratch_shapes=list(scratch),
        ),
        out_shape=out_shape,
        input_output_aliases=aliases or {},
        name=name,
        compiler_params=pltpu.CompilerParams(
            vmem_limit_bytes=vmem * 1024 * 1024,
            dimension_semantics=("arbitrary",) * len(grid),
        ),
        cost_estimate=pl.CostEstimate(flops=work, bytes_accessed=1, transcendentals=0),
    )


def whole(shape):
    return pl.BlockSpec(shape, lambda *_: (0,) * len(shape))


def part_of(place, k, cols):
    return pl.ds(pl.multiple_of((place ^ k) * cols, 128), cols)


def prep_body(count, place_ref, core_ref, chip_ref, tok_ref, gain_ref, inv_ref, out_ref):
    width = tok_ref.shape[1]
    cols = width // count
    total = jnp.zeros((tok_ref.shape[0], 1), f32)
    for k in range(count):
        x = tok_ref[:, k * cols : (k + 1) * cols].astype(f32)
        total = total + jnp.sum(x * x, axis=-1, keepdims=True)
    inverse = lax.rsqrt(total / width + norm_eps)
    inv_ref[...] = inverse
    for k in range(count):
        part = slice(k * cols, (k + 1) * cols)
        x = tok_ref[:, part].astype(f32)
        out_ref[k] = (x * inverse * gain_ref[:, part]).astype(bf16).T


def low_body(master_ref, _, low_ref):
    low_ref[...] = master_ref[...].astype(bf16)


def spread_body(count, micro, scale, place_ref, plan_ref, *refs):
    cots, (low_ref, ordered_ref), outs = refs[:count], refs[count : count + 2], refs[count + 2 :]
    rows = cots[0].shape[0]
    size = rows // micro
    for k in range(count):
        for i in range(micro):
            at = pl.multiple_of(plan_ref[i] * size, size)
            to = pl.multiple_of((place_ref[0] ^ k) * rows + i * size, size)
            ordered_ref[pl.ds(to, size), :] = cots[k][pl.ds(at, size), :]
    step = 256
    for at in range(0, low_ref.shape[0], step):
        product = lax.dot_general(
            ordered_ref[...],
            low_ref[at : at + step, :],
            (((1,), (1,)), ((), ())),
            preferred_element_type=f32,
        )
        for k in range(count):
            outs[0][k, :, at : at + step] = (product[k * rows : (k + 1) * rows, :] * scale).astype(bf16)


def grad_body(count, head, scale, owner_ref, normed_ref, *refs):
    ordered_ref, master_ref, moment_ref, second_ref, moment_out, second_out = refs[:6]
    out_ref, mark_ref, joined, fresh = refs[6:]
    tok_count = normed_ref.shape[2]
    kv_cols = master_ref.shape[1]
    mark_ref[...] = jnp.zeros_like(mark_ref)
    for k in range(count):
        joined[:, k * tok_count : (k + 1) * tok_count] = normed_ref[k]
    step = 256
    size = joined.shape[0]
    rows = pl.ds(pl.multiple_of(pl.program_id(0) * size, size), size)
    for at in range(0, kv_cols, step):
        here = slice(at, at + step)
        part = jnp.dot(joined[...], ordered_ref[:, here], preferred_element_type=f32)
        moment_new = beta_one * moment_ref[rows, here] + ((1.0 - beta_one) * scale) * part
        second_new = beta_two * second_ref[rows, here] + (
            ((1.0 - beta_two) * scale * scale) * part
        ) * part
        moment_out[:, here] = moment_new
        second_out[:, here] = second_new
        scaled = second_new * (1.0 / bias_two)
        root = scaled * lax.rsqrt(scaled) + adam_eps
        weights = master_ref[rows, here] * (1.0 - learn_rate * weight_decay) - (
            moment_new * (learn_rate / bias_one)
        ) * pl.reciprocal(root, approx=True)
        fresh[:, here] = weights.astype(bf16)
    for k in range(count):
        owner = owner_ref[k] * head
        for p in range(2):
            lanes = pl.ds(pl.multiple_of(p * (kv_cols // 2) + owner, head), head)
            out_ref[k, p * head : (p + 1) * head, :] = fresh[:, lanes].T


def own_body(core_ref, tok_ref, gain_ref, inv_ref, spread_ref, _, keep_ref, give_ref):
    core = core_ref[0]
    count, _, cols = spread_ref.shape
    half = tok_ref.shape[0] // 2
    for out_ref, pick in ((give_ref, 1 - core), (keep_ref, core)):
        rows = pl.ds(pl.multiple_of(pick * half, half), half)
        inverse = inv_ref[rows, :]
        total = jnp.zeros((half, 1), f32)
        for k in range(count):
            part = slice(k * cols, (k + 1) * cols)
            scaled = spread_ref[k, rows, :].astype(f32) * gain_ref[:, part]
            total = total + jnp.sum(
                scaled * tok_ref[rows, part].astype(f32), axis=-1, keepdims=True
            )
        factor = inverse * inverse * inverse * (total / (count * cols))
        for k in range(count):
            part = slice(k * cols, (k + 1) * cols)
            scaled = spread_ref[k, rows, :].astype(f32) * gain_ref[:, part]
            out_ref[:, part] = (
                inverse * scaled - tok_ref[rows, part].astype(f32) * factor
            ).astype(bf16)


def pair_body(chip_ref, keep_ref, got_ref, one_ref, two_ref):
    z = chip_ref[0]
    half = one_ref.shape[0]
    for out_ref, top in ((one_ref, z == 3), (two_ref, z == 2)):
        rows = pl.ds(pl.multiple_of(jnp.where(top, 0, half), half), half)
        out_ref[...] = (keep_ref[rows, :].astype(f32) + got_ref[rows, :].astype(f32)).astype(bf16)


def middle_body(chip_ref, keep_ref, got_ref, one_ref, two_ref, three_ref, four_ref):
    z = chip_ref[0]
    half = one_ref.shape[0]
    rows = pl.ds(pl.multiple_of(jnp.where(z == 2, half, 0), half), half)
    one = one_ref[...].astype(f32)
    two = two_ref[...].astype(f32)
    mine = keep_ref[rows, :].astype(f32) + got_ref[rows, :].astype(f32) + two
    three_ref[...] = (mine + jnp.where(z == 1, one, 0.0)).astype(bf16)
    four_ref[...] = (mine + one).astype(bf16)


def last_body(chip_ref, core_ref, keep_ref, got_ref, one_ref, two_ref, three_ref, four_ref, _, out_ref, send_ref):
    z = chip_ref[0]
    core = core_ref[0]
    half = one_ref.shape[0]
    for part in range(2):
        rows = slice(part * half, (part + 1) * half)
        one = one_ref[...].astype(f32)
        two = two_ref[...].astype(f32)
        three = three_ref[...].astype(f32)
        if part == 0:
            above = jnp.where(z == 1, one + two, three)
        else:
            four = four_ref[...].astype(f32)
            above = jnp.where(z == 0, four, jnp.where(z == 1, three, two))
        keep = keep_ref[rows, :].astype(f32)
        got = got_ref[rows, :].astype(f32)
        both = keep + got + above
        out_ref[rows, :] = jnp.where(core == 0, both, keep + above).astype(bf16)
        send_ref[rows, :] = jnp.where(core == 0, got + above, both).astype(bf16)


def place_body(core_ref, part_ref, *refs):
    refs[-1][...] = part_ref[...]


def rollout_body(parts_ref, out_ref, mark_ref):
    out_ref[...] = parts_ref[0]
    mark_ref[...] = jnp.zeros_like(mark_ref)


def shards(tokens, cotangents, norm_gain, master, moment, second, head_owner, plan):
    tok_rows, cot_rows = tokens[0], cotangents[0]
    master_rows, moment_rows, second_rows = master[0], moment[0], second[0]
    tok_count, width = tok_rows.shape
    kv_cols = cot_rows.shape[1]
    heads = head_owner.shape[1]
    head = kv_cols // (2 * heads)
    scale = width ** (-0.5)
    count = lax.axis_size("fsdp")
    place = lax.axis_index("fsdp").astype(jnp.int32)[None]
    section = lax.axis_index("section").astype(jnp.int32)
    core, chip = (section & 1)[None], (section >> 1)[None]
    cols = width // count
    half = tok_count // 2
    sds = jax.ShapeDtypeStruct
    dests = range(1, count)
    anywhere = pl.BlockSpec(memory_space=pl.ANY)
    resident = pl.BlockSpec(memory_space=pltpu.VMEM)
    mark = sds((8, 128), f32)

    cots = [cot_rows] + [swap(cot_rows, "fsdp", k) for k in dests]

    inverse, normed = call(
        "prep",
        functools.partial(prep_body, count),
        (1,),
        3,
        [whole((tok_count, width)), whole((1, width))],
        [whole((tok_count, 1)), whole((count, cols, tok_count))],
        [sds((tok_count, 1), f32), sds((count, cols, tok_count), bf16)],
    )(place, core, chip, tok_rows, norm_gain)
    normed = lax.all_to_all(normed, "fsdp", 0, 0, tiled=True)

    rows_step = 256
    low = call(
        "low",
        low_body,
        (cols // rows_step,),
        0,
        [pl.BlockSpec((rows_step, kv_cols), lambda i: (i, 0)), anywhere],
        pl.BlockSpec((rows_step, kv_cols), lambda i: (i, 0)),
        sds((cols, kv_cols), bf16),
    )(master_rows, inverse)
    ordered, spread = call(
        "spread",
        functools.partial(spread_body, count, plan.shape[0], scale),
        (),
        2,
        [resident] * (count + 1),
        [resident] * 2,
        [sds((count * tok_count, kv_cols), bf16), sds((count, tok_count, cols), bf16)],
        work=10**10,
    )(place, plan, *cots, low)
    spread = lax.all_to_all(spread, "fsdp", 0, 0, tiled=True)

    state = pl.BlockSpec((rows_step, kv_cols), lambda i, *_: (i, 0))
    moment_new, second_new, rollout_parts, grad_mark = call(
        "grad",
        functools.partial(grad_body, count, head, scale),
        (cols // rows_step,),
        1,
        [pl.BlockSpec((count, rows_step, tok_count), lambda i, *_: (0, i, 0))]
        + [resident, resident, resident, resident],
        [state, state]
        + [pl.BlockSpec((count, 2 * head, rows_step), lambda i, *_: (0, 0, i))]
        + [whole((8, 128))],
        [sds((cols, kv_cols), f32)] * 2 + [sds((count, 2 * head, cols), bf16), mark],
        scratch=[
            pltpu.VMEM((rows_step, count * tok_count), bf16),
            pltpu.VMEM((rows_step, kv_cols), bf16),
        ],
        vmem=20,
    )(head_owner[0], normed, ordered, master_rows, moment_rows, second_rows)

    rollout, rollout_mark = call(
        "rollout",
        rollout_body,
        (count,),
        0,
        [pl.BlockSpec((1, 2 * head, cols), lambda k: (k, 0, 0))],
        [pl.BlockSpec((2 * head, cols), lambda k: (0, k)), whole((8, 128))],
        [sds((2 * head, width), bf16), mark],
        work=10**9,
    )(lax.all_to_all(rollout_parts, "fsdp", 0, 0, tiled=True))

    keep, give = call(
        "own",
        own_body,
        (1,),
        1,
        [whole((tok_count, width)), whole((1, width)), whole((tok_count, 1))]
        + [whole((count, tok_count, cols)), anywhere],
        [whole((half, width))] * 2,
        [sds((half, width), bf16)] * 2,
    )(core, tok_rows, norm_gain, inverse, spread, grad_mark)
    got = swap(give, "section", 1)

    def chips(pairs):
        return [(2 * a + c, 2 * b + c) for c in range(2) for a, b in pairs]

    quarter = half // 2
    full, part = whole((half, width)), whole((quarter, width))
    piece = sds((quarter, width), bf16)
    one, two = call("pair", pair_body, (1,), 1, [full, full], [part, part], [piece, piece])(
        chip, keep, got
    )
    one = lax.ppermute(one, "section", chips([(3, 1), (1, 2)]))
    two = lax.ppermute(two, "section", chips([(2, 1), (3, 2)]))
    three, four = call(
        "middle", middle_body, (1,), 1, [full, full, part, part], [part, part], [piece, piece]
    )(chip, keep, got, one, two)
    three = lax.ppermute(three, "section", chips([(1, 0), (2, 1), (3, 2)]))
    four = lax.ppermute(four, "section", chips([(2, 0)]))
    grads, send = call(
        "last",
        last_body,
        (1,),
        2,
        [full, full, part, part, part, part, anywhere],
        [pl.BlockSpec((half, width), lambda i, chip_ref, core_ref: (core_ref[0], 0)), full],
        [sds((tok_count, width), bf16), sds((half, width), bf16)],
    )(chip, core, keep, got, one, two, three, four, rollout_mark)
    other = swap(send, "section", 1)
    grads = call(
        "join",
        place_body,
        (1,),
        1,
        [full, anywhere],
        pl.BlockSpec((half, width), lambda i, core_ref: (1 - core_ref[0], 0)),
        sds((tok_count, width), bf16),
        aliases={2: 0},
    )(core, other, grads)
    return (grads[None], moment_new[None], second_new[None], rollout[None])


def choose(*args):
    tokens, cotangents, norm_gain, master, moment, second, head_owner, plan = args
    count, sections = lax.axis_size("fsdp"), lax.axis_size("section")
    tok_count, width = tokens.shape[1:]
    kv_cols, heads = cotangents.shape[2], head_owner.shape[1]
    fits = (
        count == 4
        and sections == 8
        and heads == count
        and plan.shape[0] == 4
        and kv_cols == 2 * heads * 128
        and (width // count) % 256 == 0
        and tok_count % 128 == 0
        and tok_count % (16 * plan.shape[0]) == 0
    )
    return (shards if fits else shards_any)(*args)


def solution(mesh):
    in_specs = (
        P("section", "fsdp", None),
        P("section", "fsdp", None),
        P("section", None),
        P("section", "fsdp", None),
        P("section", "fsdp", None),
        P("section", "fsdp", None),
        P("section", None),
        P(),
    )
    out_specs = (
        P("section", "fsdp", None),
        P("section", "fsdp", None),
        P("section", "fsdp", None),
        P("section", "fsdp", None),
    )
    return jax.shard_map(choose, mesh=mesh, in_specs=in_specs, out_specs=out_specs, check_vma=False)
```

```python
import functools

import jax
import jax.numpy as jnp
from jax import lax
from jax.experimental import pallas as pl
from jax.experimental.pallas import tpu as pltpu
from jax.sharding import PartitionSpec as P

beta_one = 0.9
beta_two = 0.95
bias_one = 1.0 - 0.9**10
bias_two = 1.0 - 0.95**10
adam_eps = 1e-08
learn_rate = 0.02
weight_decay = 0.1
norm_eps = 1e-06

bf16 = jnp.bfloat16
f32 = jnp.float32


def swap(x, axis, k):
    count = lax.axis_size(axis)
    return lax.ppermute(x, axis, [(i, i ^ k) for i in range(count)])


def adam_step(master, moment, second, gradient):
    moment_new = beta_one * moment + (1.0 - beta_one) * gradient
    second_new = beta_two * second + (1.0 - beta_two) * gradient * gradient
    update = moment_new / bias_one / (jnp.sqrt(second_new / bias_two) + adam_eps)
    weights = master - learn_rate * (update + weight_decay * master)
    return (moment_new, second_new, weights)


def plan_rows(cot_rows, plan):
    micro_count = plan.shape[0]
    blocks = cot_rows.reshape(micro_count, -1, cot_rows.shape[-1])
    return jnp.take(blocks, plan, axis=0).reshape(cot_rows.shape)


def suffix_sum(own_term, axis):
    count = lax.axis_size(axis)
    place = lax.axis_index(axis)
    low = own_term.astype(bf16)
    pair = lax.ppermute(low, axis, [(i + 1, i) for i in range(0, count, 2)])
    total = own_term + pair.astype(f32)
    above = jnp.zeros_like(low)
    for z in range(count // 2 - 1, 0, -1):
        got = lax.ppermute(total.astype(bf16), axis, [(2 * z, 2 * z - 2)])
        total = total + got.astype(f32)
        above = above + got
    from_pair = lax.ppermute(above, axis, [(i, i + 1) for i in range(0, count, 2)])
    return jnp.where(place % 2 == 0, total, own_term + from_pair.astype(f32))


def shards_any(tokens, cotangents, norm_gain, master, moment, second, head_owner, plan):
    tok_rows = tokens[0]
    gain_row = norm_gain[0]
    master_rows = master[0]
    owner_row = head_owner[0]
    width = tok_rows.shape[1]
    tok_count = tok_rows.shape[0]
    proj_scale = width ** (-0.5)
    count = lax.axis_size("fsdp")
    place = lax.axis_index("fsdp")
    cols = width // count

    def block_of(x, k):
        return lax.dynamic_slice_in_dim(x, (place ^ k) * cols, cols, axis=-1)

    ordered = plan_rows(cotangents[0], plan)
    all_ordered = [ordered] + [swap(ordered, "fsdp", k) for k in range(1, count)]
    widened = tok_rows.astype(f32)
    inverse = lax.rsqrt(jnp.mean(widened * widened, axis=-1, keepdims=True) + norm_eps)
    normed = (widened * inverse * gain_row).astype(bf16)
    all_normed = [block_of(normed, 0)] + [
        swap(block_of(normed, k), "fsdp", k) for k in range(1, count)
    ]
    low_weights = master_rows.astype(bf16)
    spread = []
    for k in range(count):
        part = (
            jnp.einsum("tc,rc->tr", all_ordered[k], low_weights, preferred_element_type=f32)
            * proj_scale
        )
        spread.append(part if k == 0 else swap(part.astype(bf16), "fsdp", k).astype(f32))

    gradient = (
        jnp.einsum(
            "td,tc->dc",
            jnp.concatenate(all_normed, axis=0),
            jnp.concatenate(all_ordered, axis=0),
            preferred_element_type=f32,
        )
        * proj_scale
    )
    moment_new, second_new, weights = adam_step(master_rows, moment[0], second[0], gradient)
    heads = owner_row.shape[0]
    low_new = weights.astype(bf16).reshape(cols, 2, heads, -1)
    arranged = jnp.take(low_new, owner_row, axis=2).transpose(2, 1, 3, 0).reshape(count, -1, cols)
    rollout = jnp.zeros((arranged.shape[1], width), bf16)
    for k in range(count):
        part = lax.dynamic_index_in_dim(arranged, place ^ k, 0, False)
        if k:
            part = swap(part, "fsdp", k)
        rollout = lax.dynamic_update_slice_in_dim(rollout, part, (place ^ k) * cols, axis=1)

    tok_k = [block_of(tok_rows, k).astype(f32) for k in range(count)]
    scaled = [spread[k] * block_of(gain_row, k) for k in range(count)]
    mean_term = sum(jnp.sum(scaled[k] * tok_k[k], axis=-1, keepdims=True) for k in range(count)) / width
    factor = inverse * inverse * inverse * mean_term
    own_term = jnp.concatenate(
        [inverse * scaled[k] - tok_k[k] * factor for k in range(count)], axis=0
    )
    summed = suffix_sum(own_term, "section").astype(bf16).reshape(count, tok_count, cols)
    input_grads = jnp.zeros((tok_count, width), bf16)
    for k in range(count):
        input_grads = lax.dynamic_update_slice_in_dim(
            input_grads, summed[k], (place ^ k) * cols, axis=1
        )
    return (input_grads[None], moment_new[None], second_new[None], rollout[None])


def call(name, body, grid, prefetch, in_specs, out_specs, out_shape, scratch=(), aliases=None, vmem=16, work=1):
    return pl.pallas_call(
        body,
        grid_spec=pltpu.PrefetchScalarGridSpec(
            num_scalar_prefetch=prefetch,
            grid=grid,
            in_specs=in_specs,
            out_specs=out_specs,
            scratch_shapes=list(scratch),
        ),
        out_shape=out_shape,
        input_output_aliases=aliases or {},
        name=name,
        compiler_params=pltpu.CompilerParams(
            vmem_limit_bytes=vmem * 1024 * 1024,
            dimension_semantics=("arbitrary",) * len(grid),
        ),
        cost_estimate=pl.CostEstimate(flops=work, bytes_accessed=1, transcendentals=0),
    )


def whole(shape):
    return pl.BlockSpec(shape, lambda *_: (0,) * len(shape))


def part_of(place, k, cols):
    return pl.ds(pl.multiple_of((place ^ k) * cols, 128), cols)


def prep_body(count, place_ref, core_ref, chip_ref, tok_ref, gain_ref, inv_ref, *out_refs):
    place = place_ref[0]
    width = tok_ref.shape[1]
    cols = width // count
    total = jnp.zeros((tok_ref.shape[0], 1), f32)
    for k in range(count):
        x = tok_ref[:, k * cols : (k + 1) * cols].astype(f32)
        total = total + jnp.sum(x * x, axis=-1, keepdims=True)
    inverse = lax.rsqrt(total / width + norm_eps)
    inv_ref[...] = inverse
    for k in range(count):
        part = part_of(place, k, cols)
        x = tok_ref[:, part].astype(f32)
        out_refs[k][...] = (x * inverse * gain_ref[:, part]).astype(bf16).T


def low_body(master_ref, _, low_ref):
    low_ref[...] = master_ref[...].astype(bf16)


def spread_body(count, micro, scale, plan_ref, *refs):
    cots, (low_ref, ordered_ref), outs = refs[:count], refs[count : count + 2], refs[count + 2 :]
    rows = cots[0].shape[0]
    size = rows // micro
    for k in range(count):
        for i in range(micro):
            at = pl.multiple_of(plan_ref[i] * size, size)
            ordered_ref[k * rows + i * size : k * rows + (i + 1) * size, :] = cots[k][
                pl.ds(at, size), :
            ]
    step = 256
    for at in range(0, low_ref.shape[0], step):
        product = lax.dot_general(
            ordered_ref[...],
            low_ref[at : at + step, :],
            (((1,), (1,)), ((), ())),
            preferred_element_type=f32,
        )
        for k in range(count):
            outs[k][:, at : at + step] = (product[k * rows : (k + 1) * rows, :] * scale).astype(bf16)


def grad_body(count, head, scale, place_ref, owner_ref, *refs):
    normed, refs = refs[:count], refs[count:]
    ordered_ref, master_ref, moment_ref, second_ref, moment_out, second_out = refs[:6]
    outs, mark_ref, joined, fresh = refs[6 : 6 + count], *refs[6 + count :]
    tok_count = normed[0].shape[1]
    kv_cols = master_ref.shape[1]
    mark_ref[...] = jnp.zeros_like(mark_ref)
    for k in range(count):
        joined[:, k * tok_count : (k + 1) * tok_count] = normed[k][...]
    step = 256
    size = joined.shape[0]
    rows = pl.ds(pl.multiple_of(pl.program_id(0) * size, size), size)
    for at in range(0, kv_cols, step):
        here = slice(at, at + step)
        part = jnp.dot(joined[...], ordered_ref[:, here], preferred_element_type=f32)
        moment_new = beta_one * moment_ref[rows, here] + ((1.0 - beta_one) * scale) * part
        second_new = beta_two * second_ref[rows, here] + (
            ((1.0 - beta_two) * scale * scale) * part
        ) * part
        moment_out[:, here] = moment_new
        second_out[:, here] = second_new
        scaled = second_new * (1.0 / bias_two)
        root = scaled * lax.rsqrt(scaled) + adam_eps
        weights = master_ref[rows, here] * (1.0 - learn_rate * weight_decay) - (
            moment_new * (learn_rate / bias_one)
        ) * pl.reciprocal(root, approx=True)
        fresh[:, here] = weights.astype(bf16)
    for k in range(count):
        owner = owner_ref[place_ref[0] ^ k] * head
        for p in range(2):
            lanes = pl.ds(pl.multiple_of(p * (kv_cols // 2) + owner, head), head)
            outs[k][p * head : (p + 1) * head, :] = fresh[:, lanes].T


def own_body(count, mine, place_ref, core_ref, tok_ref, gain_ref, inv_ref, *refs):
    spread, out_ref = refs[:count], refs[-1]
    place = place_ref[0]
    core = core_ref[0]
    width = tok_ref.shape[1]
    cols = width // count
    half = tok_ref.shape[0] // 2
    pick = core if mine else 1 - core
    rows = pl.ds(pl.multiple_of(pick * half, half), half)
    inverse = inv_ref[rows, :]
    total = jnp.zeros((half, 1), f32)
    for k in range(count):
        part = part_of(place, k, cols)
        scaled = spread[k][rows, :].astype(f32) * gain_ref[:, part]
        total = total + jnp.sum(
            scaled * tok_ref[rows, part].astype(f32), axis=-1, keepdims=True
        )
    factor = inverse * inverse * inverse * (total / width)
    for k in range(count):
        part = part_of(place, k, cols)
        scaled = spread[k][rows, :].astype(f32) * gain_ref[:, part]
        out_ref[:, part] = (
            inverse * scaled - tok_ref[rows, part].astype(f32) * factor
        ).astype(bf16)


def pair_body(chip_ref, keep_ref, got_ref, one_ref, two_ref):
    z = chip_ref[0]
    half = one_ref.shape[0]
    for out_ref, top in ((one_ref, z == 3), (two_ref, z == 2)):
        rows = pl.ds(pl.multiple_of(jnp.where(top, 0, half), half), half)
        out_ref[...] = (keep_ref[rows, :].astype(f32) + got_ref[rows, :].astype(f32)).astype(bf16)


def middle_body(chip_ref, keep_ref, got_ref, one_ref, two_ref, three_ref, four_ref):
    z = chip_ref[0]
    half = one_ref.shape[0]
    rows = pl.ds(pl.multiple_of(jnp.where(z == 2, half, 0), half), half)
    one = one_ref[...].astype(f32)
    two = two_ref[...].astype(f32)
    mine = keep_ref[rows, :].astype(f32) + got_ref[rows, :].astype(f32) + two
    three_ref[...] = (mine + jnp.where(z == 1, one, 0.0)).astype(bf16)
    four_ref[...] = (mine + one).astype(bf16)


def last_body(mine, chip_ref, core_ref, keep_ref, got_ref, one_ref, two_ref, three_ref, four_ref, _, out_ref):
    z = chip_ref[0]
    lower = (core_ref[0] == 0) == mine
    half = one_ref.shape[0]
    kept, came = (keep_ref, got_ref) if mine else (got_ref, keep_ref)
    for part in range(2):
        rows = slice(part * half, (part + 1) * half)
        one = one_ref[...].astype(f32)
        two = two_ref[...].astype(f32)
        three = three_ref[...].astype(f32)
        if part == 0:
            above = jnp.where(z == 1, one + two, three)
        else:
            four = four_ref[...].astype(f32)
            above = jnp.where(z == 0, four, jnp.where(z == 1, three, two))
        total = kept[rows, :].astype(f32) + above
        both = total + came[rows, :].astype(f32)
        out_ref[rows, :] = jnp.where(lower, both, total).astype(bf16)


def place_body(place_ref, part_ref, *refs):
    refs[-1][...] = part_ref[...]


def marked_body(place_ref, part_ref, _, out_ref, mark_ref):
    out_ref[...] = part_ref[...]
    mark_ref[...] = jnp.zeros_like(mark_ref)


def shards(tokens, cotangents, norm_gain, master, moment, second, head_owner, plan):
    tok_rows, cot_rows = tokens[0], cotangents[0]
    master_rows, moment_rows, second_rows = master[0], moment[0], second[0]
    tok_count, width = tok_rows.shape
    kv_cols = cot_rows.shape[1]
    heads = head_owner.shape[1]
    head = kv_cols // (2 * heads)
    scale = width ** (-0.5)
    count = lax.axis_size("fsdp")
    place = lax.axis_index("fsdp").astype(jnp.int32)[None]
    section = lax.axis_index("section").astype(jnp.int32)
    core, chip = (section & 1)[None], (section >> 1)[None]
    cols = width // count
    half = tok_count // 2
    sds = jax.ShapeDtypeStruct
    dests = range(1, count)
    anywhere = pl.BlockSpec(memory_space=pl.ANY)
    resident = pl.BlockSpec(memory_space=pltpu.VMEM)
    mark = sds((8, 128), f32)

    cots = [cot_rows] + [swap(cot_rows, "fsdp", k) for k in dests]

    inverse, *normed = call(
        "prep",
        functools.partial(prep_body, count),
        (1,),
        3,
        [whole((tok_count, width)), whole((1, width))],
        [whole((tok_count, 1))] + [whole((cols, tok_count))] * count,
        [sds((tok_count, 1), f32)] + [sds((cols, tok_count), bf16)] * count,
    )(place, core, chip, tok_rows, norm_gain)
    normed = [normed[0]] + [swap(normed[k], "fsdp", k) for k in dests]

    rows_step = 256
    low = call(
        "low",
        low_body,
        (cols // rows_step,),
        0,
        [pl.BlockSpec((rows_step, kv_cols), lambda i: (i, 0)), anywhere],
        pl.BlockSpec((rows_step, kv_cols), lambda i: (i, 0)),
        sds((cols, kv_cols), bf16),
    )(master_rows, inverse)
    ordered, *spread = call(
        "spread",
        functools.partial(spread_body, count, plan.shape[0], scale),
        (),
        1,
        [resident] * (count + 1),
        [resident] * (count + 1),
        [sds((count * tok_count, kv_cols), bf16)] + [sds((tok_count, cols), bf16)] * count,
        work=10**10,
    )(plan, *cots, low)
    spread = [spread[0]] + [swap(spread[k], "fsdp", k) for k in dests]

    state = pl.BlockSpec((rows_step, kv_cols), lambda i, *_: (i, 0))
    moment_new, second_new, *rollout_parts, grad_mark = call(
        "grad",
        functools.partial(grad_body, count, head, scale),
        (cols // rows_step,),
        2,
        [pl.BlockSpec((rows_step, tok_count), lambda i, *_: (i, 0))] * count
        + [resident, resident, resident, resident],
        [state, state]
        + [pl.BlockSpec((2 * head, rows_step), lambda i, *_: (0, i))] * count
        + [whole((8, 128))],
        [sds((cols, kv_cols), f32)] * 2 + [sds((2 * head, cols), bf16)] * count + [mark],
        scratch=[
            pltpu.VMEM((rows_step, count * tok_count), bf16),
            pltpu.VMEM((rows_step, kv_cols), bf16),
        ],
        vmem=20,
    )(place, head_owner[0], *normed, ordered, master_rows, moment_rows, second_rows)

    rollout = ()
    rollout_mark = ()
    for k in (0, 3, 1, 2):
        part = swap(rollout_parts[k], "fsdp", k) if k else rollout_parts[k]
        final = k == 2
        rollout, *rollout_mark = call(
            "place",
            marked_body if final else place_body,
            (1,),
            1,
            [whole((2 * head, cols))] + ([anywhere] if k else []),
            [pl.BlockSpec((2 * head, cols), lambda i, place_ref, k=k: (0, place_ref[0] ^ k))]
            + ([whole((8, 128))] if final else []),
            [sds((2 * head, width), bf16)] + ([mark] if final else []),
            aliases={2: 0} if k else None,
            work=1,
        )(place, part, *([rollout] if k else []))

    def own(name, mine, after):
        (term,) = call(
            name,
            functools.partial(own_body, count, mine),
            (1,),
            2,
            [whole((tok_count, width)), whole((1, width)), whole((tok_count, 1))]
            + [whole((tok_count, cols))] * count
            + [anywhere],
            [whole((half, width))],
            [sds((half, width), bf16)],
        )(place, core, tok_rows, norm_gain, inverse, *spread, after)
        return term

    give = own("own", False, grad_mark)
    keep = own("keep", True, give)
    got = swap(give, "section", 1)

    def chips(pairs):
        return [(2 * a + c, 2 * b + c) for c in range(2) for a, b in pairs]

    quarter = half // 2
    full, part = whole((half, width)), whole((quarter, width))
    piece = sds((quarter, width), bf16)
    one, two = call("pair", pair_body, (1,), 1, [full, full], [part, part], [piece, piece])(
        chip, keep, got
    )
    one = lax.ppermute(one, "section", chips([(3, 1), (1, 2)]))
    two = lax.ppermute(two, "section", chips([(2, 1), (3, 2)]))
    three, four = call(
        "middle", middle_body, (1,), 1, [full, full, part, part], [part, part], [piece, piece]
    )(chip, keep, got, one, two)
    three = lax.ppermute(three, "section", chips([(1, 0), (2, 1), (3, 2)]))
    four = lax.ppermute(four, "section", chips([(2, 0)]))
    terms = (chip, core, keep, got, one, two, three, four)
    shapes = [full, full, part, part, part, part, anywhere]
    (send,) = call(
        "last",
        functools.partial(last_body, False),
        (1,),
        2,
        shapes,
        [full],
        [sds((half, width), bf16)],
    )(*terms, *rollout_mark)
    other = swap(send, "section", 1)
    (grads,) = call(
        "mine",
        functools.partial(last_body, True),
        (1,),
        2,
        shapes,
        [pl.BlockSpec((half, width), lambda i, chip_ref, core_ref: (core_ref[0], 0))],
        [sds((tok_count, width), bf16)],
    )(*terms, send)
    grads = call(
        "join",
        place_body,
        (1,),
        1,
        [full, anywhere],
        pl.BlockSpec((half, width), lambda i, core_ref: (1 - core_ref[0], 0)),
        sds((tok_count, width), bf16),
        aliases={2: 0},
    )(core, other, grads)
    return (grads[None], moment_new[None], second_new[None], rollout[None])


def choose(*args):
    tokens, cotangents, norm_gain, master, moment, second, head_owner, plan = args
    count, sections = lax.axis_size("fsdp"), lax.axis_size("section")
    tok_count, width = tokens.shape[1:]
    kv_cols, heads = cotangents.shape[2], head_owner.shape[1]
    fits = (
        count == 4
        and sections == 8
        and heads == count
        and plan.shape[0] == 4
        and kv_cols == 2 * heads * 128
        and (width // count) % 256 == 0
        and tok_count % 128 == 0
        and tok_count % (16 * plan.shape[0]) == 0
    )
    return (shards if fits else shards_any)(*args)


def solution(mesh):
    in_specs = (
        P("section", "fsdp", None),
        P("section", "fsdp", None),
        P("section", None),
        P("section", "fsdp", None),
        P("section", "fsdp", None),
        P("section", "fsdp", None),
        P("section", None),
        P(),
    )
    out_specs = (
        P("section", "fsdp", None),
        P("section", "fsdp", None),
        P("section", "fsdp", None),
        P("section", "fsdp", None),
    )
    return jax.shard_map(choose, mesh=mesh, in_specs=in_specs, out_specs=out_specs, check_vma=False)
```

```python
import functools

import jax
import jax.numpy as jnp
from jax import lax
from jax.experimental import pallas as pl
from jax.experimental.pallas import tpu as pltpu
from jax.sharding import PartitionSpec as P

beta_one = 0.9
beta_two = 0.95
bias_one = 1.0 - 0.9**10
bias_two = 1.0 - 0.95**10
adam_eps = 1e-08
learn_rate = 0.02
weight_decay = 0.1
norm_eps = 1e-06

bf16 = jnp.bfloat16
f32 = jnp.float32


def swap(x, axis, k):
    count = lax.axis_size(axis)
    return lax.ppermute(x, axis, [(i, i ^ k) for i in range(count)])


def adam_step(master, moment, second, gradient):
    moment_new = beta_one * moment + (1.0 - beta_one) * gradient
    second_new = beta_two * second + (1.0 - beta_two) * gradient * gradient
    update = moment_new / bias_one / (jnp.sqrt(second_new / bias_two) + adam_eps)
    weights = master - learn_rate * (update + weight_decay * master)
    return (moment_new, second_new, weights)


def plan_rows(cot_rows, plan):
    micro_count = plan.shape[0]
    blocks = cot_rows.reshape(micro_count, -1, cot_rows.shape[-1])
    return jnp.take(blocks, plan, axis=0).reshape(cot_rows.shape)


def suffix_sum(own_term, axis):
    count = lax.axis_size(axis)
    place = lax.axis_index(axis)
    low = own_term.astype(bf16)
    pair = lax.ppermute(low, axis, [(i + 1, i) for i in range(0, count, 2)])
    total = own_term + pair.astype(f32)
    above = jnp.zeros_like(low)
    for z in range(count // 2 - 1, 0, -1):
        got = lax.ppermute(total.astype(bf16), axis, [(2 * z, 2 * z - 2)])
        total = total + got.astype(f32)
        above = above + got
    from_pair = lax.ppermute(above, axis, [(i, i + 1) for i in range(0, count, 2)])
    return jnp.where(place % 2 == 0, total, own_term + from_pair.astype(f32))


def shards_any(tokens, cotangents, norm_gain, master, moment, second, head_owner, plan):
    tok_rows = tokens[0]
    gain_row = norm_gain[0]
    master_rows = master[0]
    owner_row = head_owner[0]
    width = tok_rows.shape[1]
    tok_count = tok_rows.shape[0]
    proj_scale = width ** (-0.5)
    count = lax.axis_size("fsdp")
    place = lax.axis_index("fsdp")
    cols = width // count

    def block_of(x, k):
        return lax.dynamic_slice_in_dim(x, (place ^ k) * cols, cols, axis=-1)

    ordered = plan_rows(cotangents[0], plan)
    all_ordered = [ordered] + [swap(ordered, "fsdp", k) for k in range(1, count)]
    widened = tok_rows.astype(f32)
    inverse = lax.rsqrt(jnp.mean(widened * widened, axis=-1, keepdims=True) + norm_eps)
    normed = (widened * inverse * gain_row).astype(bf16)
    all_normed = [block_of(normed, 0)] + [
        swap(block_of(normed, k), "fsdp", k) for k in range(1, count)
    ]
    low_weights = master_rows.astype(bf16)
    spread = []
    for k in range(count):
        part = (
            jnp.einsum("tc,rc->tr", all_ordered[k], low_weights, preferred_element_type=f32)
            * proj_scale
        )
        spread.append(part if k == 0 else swap(part.astype(bf16), "fsdp", k).astype(f32))

    gradient = (
        jnp.einsum(
            "td,tc->dc",
            jnp.concatenate(all_normed, axis=0),
            jnp.concatenate(all_ordered, axis=0),
            preferred_element_type=f32,
        )
        * proj_scale
    )
    moment_new, second_new, weights = adam_step(master_rows, moment[0], second[0], gradient)
    heads = owner_row.shape[0]
    low_new = weights.astype(bf16).reshape(cols, 2, heads, -1)
    arranged = jnp.take(low_new, owner_row, axis=2).transpose(2, 1, 3, 0).reshape(count, -1, cols)
    rollout = jnp.zeros((arranged.shape[1], width), bf16)
    for k in range(count):
        part = lax.dynamic_index_in_dim(arranged, place ^ k, 0, False)
        if k:
            part = swap(part, "fsdp", k)
        rollout = lax.dynamic_update_slice_in_dim(rollout, part, (place ^ k) * cols, axis=1)

    tok_k = [block_of(tok_rows, k).astype(f32) for k in range(count)]
    scaled = [spread[k] * block_of(gain_row, k) for k in range(count)]
    mean_term = sum(jnp.sum(scaled[k] * tok_k[k], axis=-1, keepdims=True) for k in range(count)) / width
    factor = inverse * inverse * inverse * mean_term
    own_term = jnp.concatenate(
        [inverse * scaled[k] - tok_k[k] * factor for k in range(count)], axis=0
    )
    summed = suffix_sum(own_term, "section").astype(bf16).reshape(count, tok_count, cols)
    input_grads = jnp.zeros((tok_count, width), bf16)
    for k in range(count):
        input_grads = lax.dynamic_update_slice_in_dim(
            input_grads, summed[k], (place ^ k) * cols, axis=1
        )
    return (input_grads[None], moment_new[None], second_new[None], rollout[None])


def call(name, body, grid, prefetch, in_specs, out_specs, out_shape, scratch=(), aliases=None, vmem=16, work=1):
    return pl.pallas_call(
        body,
        grid_spec=pltpu.PrefetchScalarGridSpec(
            num_scalar_prefetch=prefetch,
            grid=grid,
            in_specs=in_specs,
            out_specs=out_specs,
            scratch_shapes=list(scratch),
        ),
        out_shape=out_shape,
        input_output_aliases=aliases or {},
        name=name,
        compiler_params=pltpu.CompilerParams(
            vmem_limit_bytes=vmem * 1024 * 1024,
            dimension_semantics=("arbitrary",) * len(grid),
        ),
        cost_estimate=pl.CostEstimate(flops=work, bytes_accessed=1, transcendentals=0),
    )


def whole(shape):
    return pl.BlockSpec(shape, lambda *_: (0,) * len(shape))


def part_of(place, k, cols):
    return pl.ds(pl.multiple_of((place ^ k) * cols, 128), cols)


def prep_body(count, place_ref, core_ref, chip_ref, tok_ref, gain_ref, inv_ref, *out_refs):
    place = place_ref[0]
    width = tok_ref.shape[1]
    cols = width // count
    total = jnp.zeros((tok_ref.shape[0], 1), f32)
    for k in range(count):
        x = tok_ref[:, k * cols : (k + 1) * cols].astype(f32)
        total = total + jnp.sum(x * x, axis=-1, keepdims=True)
    inverse = lax.rsqrt(total / width + norm_eps)
    inv_ref[...] = inverse
    for k in range(count):
        part = part_of(place, k, cols)
        x = tok_ref[:, part].astype(f32)
        out_refs[k][...] = (x * inverse * gain_ref[:, part]).astype(bf16).T


def low_body(master_ref, _, low_ref):
    low_ref[...] = master_ref[...].astype(bf16)


def spread_body(count, micro, scale, plan_ref, *refs):
    cots, (low_ref, ordered_ref), outs = refs[:count][::-1], refs[count : count + 2], refs[count + 2 :]
    rows = cots[0].shape[0]
    size = rows // micro
    for k in range(count):
        for i in range(micro):
            at = pl.multiple_of(plan_ref[i] * size, size)
            ordered_ref[k * rows + i * size : k * rows + (i + 1) * size, :] = cots[k][
                pl.ds(at, size), :
            ]
    step = 256
    for at in range(0, low_ref.shape[0], step):
        product = lax.dot_general(
            ordered_ref[...],
            low_ref[at : at + step, :],
            (((1,), (1,)), ((), ())),
            preferred_element_type=f32,
        )
        for k in range(count):
            outs[k][:, at : at + step] = (product[k * rows : (k + 1) * rows, :] * scale).astype(bf16)


def grad_body(count, head, scale, place_ref, owner_ref, *refs):
    normed, refs = refs[:count][::-1], refs[count:]
    ordered_ref, master_ref, moment_ref, second_ref, moment_out, second_out = refs[:6]
    outs, mark_ref, joined, fresh = refs[6 : 6 + count], *refs[6 + count :]
    tok_count = normed[0].shape[1]
    kv_cols = master_ref.shape[1]
    mark_ref[...] = jnp.zeros_like(mark_ref)
    for k in range(count):
        joined[:, k * tok_count : (k + 1) * tok_count] = normed[k][...]
    step = 256
    size = joined.shape[0]
    rows = pl.ds(pl.multiple_of(pl.program_id(0) * size, size), size)
    for at in range(0, kv_cols, step):
        here = slice(at, at + step)
        part = jnp.dot(joined[...], ordered_ref[:, here], preferred_element_type=f32)
        moment_new = beta_one * moment_ref[rows, here] + ((1.0 - beta_one) * scale) * part
        second_new = beta_two * second_ref[rows, here] + (
            ((1.0 - beta_two) * scale * scale) * part
        ) * part
        moment_out[:, here] = moment_new
        second_out[:, here] = second_new
        scaled = second_new * (1.0 / bias_two)
        root = scaled * lax.rsqrt(scaled) + adam_eps
        weights = master_ref[rows, here] * (1.0 - learn_rate * weight_decay) - (
            moment_new * (learn_rate / bias_one)
        ) * pl.reciprocal(root, approx=True)
        fresh[:, here] = weights.astype(bf16)
    for k in range(count):
        owner = owner_ref[place_ref[0] ^ k] * head
        for p in range(2):
            lanes = pl.ds(pl.multiple_of(p * (kv_cols // 2) + owner, head), head)
            outs[k][p * head : (p + 1) * head, :] = fresh[:, lanes].T


def own_body(count, mine, place_ref, core_ref, tok_ref, gain_ref, inv_ref, *refs):
    spread, out_ref = refs[:count][::-1], refs[-1]
    place = place_ref[0]
    core = core_ref[0]
    width = tok_ref.shape[1]
    cols = width // count
    half = tok_ref.shape[0] // 2
    pick = core if mine else 1 - core
    rows = pl.ds(pl.multiple_of(pick * half, half), half)
    inverse = inv_ref[rows, :]
    total = jnp.zeros((half, 1), f32)
    for k in range(count):
        part = part_of(place, k, cols)
        scaled = spread[k][rows, :].astype(f32) * gain_ref[:, part]
        total = total + jnp.sum(
            scaled * tok_ref[rows, part].astype(f32), axis=-1, keepdims=True
        )
    factor = inverse * inverse * inverse * (total / width)
    for k in range(count):
        part = part_of(place, k, cols)
        scaled = spread[k][rows, :].astype(f32) * gain_ref[:, part]
        out_ref[:, part] = (
            inverse * scaled - tok_ref[rows, part].astype(f32) * factor
        ).astype(bf16)


def pair_body(chip_ref, keep_ref, got_ref, one_ref, two_ref):
    z = chip_ref[0]
    half = one_ref.shape[0]
    for out_ref, top in ((one_ref, z == 3), (two_ref, z == 2)):
        rows = pl.ds(pl.multiple_of(jnp.where(top, 0, half), half), half)
        out_ref[...] = (keep_ref[rows, :].astype(f32) + got_ref[rows, :].astype(f32)).astype(bf16)


def middle_body(chip_ref, keep_ref, got_ref, two_ref, one_ref, three_ref, four_ref):
    z = chip_ref[0]
    half = one_ref.shape[0]
    rows = pl.ds(pl.multiple_of(jnp.where(z == 2, half, 0), half), half)
    one = one_ref[...].astype(f32)
    two = two_ref[...].astype(f32)
    mine = keep_ref[rows, :].astype(f32) + got_ref[rows, :].astype(f32) + two
    three_ref[...] = (mine + jnp.where(z == 1, one, 0.0)).astype(bf16)
    four_ref[...] = (mine + one).astype(bf16)


def last_body(mine, chip_ref, core_ref, keep_ref, got_ref, two_ref, one_ref, four_ref, three_ref, _, out_ref):
    z = chip_ref[0]
    lower = (core_ref[0] == 0) == mine
    half = one_ref.shape[0]
    kept, came = (keep_ref, got_ref) if mine else (got_ref, keep_ref)
    for part in range(2):
        rows = slice(part * half, (part + 1) * half)
        one = one_ref[...].astype(f32)
        two = two_ref[...].astype(f32)
        three = three_ref[...].astype(f32)
        if part == 0:
            above = jnp.where(z == 1, one + two, three)
        else:
            four = four_ref[...].astype(f32)
            above = jnp.where(z == 0, four, jnp.where(z == 1, three, two))
        total = kept[rows, :].astype(f32) + above
        both = total + came[rows, :].astype(f32)
        out_ref[rows, :] = jnp.where(lower, both, total).astype(bf16)


def place_body(place_ref, part_ref, *refs):
    refs[-1][...] = part_ref[...]


def marked_body(place_ref, part_ref, _, out_ref, mark_ref):
    out_ref[...] = part_ref[...]
    mark_ref[...] = jnp.zeros_like(mark_ref)


def shards(tokens, cotangents, norm_gain, master, moment, second, head_owner, plan):
    tok_rows, cot_rows = tokens[0], cotangents[0]
    master_rows, moment_rows, second_rows = master[0], moment[0], second[0]
    tok_count, width = tok_rows.shape
    kv_cols = cot_rows.shape[1]
    heads = head_owner.shape[1]
    head = kv_cols // (2 * heads)
    scale = width ** (-0.5)
    count = lax.axis_size("fsdp")
    place = lax.axis_index("fsdp").astype(jnp.int32)[None]
    section = lax.axis_index("section").astype(jnp.int32)
    core, chip = (section & 1)[None], (section >> 1)[None]
    cols = width // count
    half = tok_count // 2
    sds = jax.ShapeDtypeStruct
    dests = range(1, count)
    anywhere = pl.BlockSpec(memory_space=pl.ANY)
    resident = pl.BlockSpec(memory_space=pltpu.VMEM)
    mark = sds((8, 128), f32)

    cots = [cot_rows] + [swap(cot_rows, "fsdp", k) for k in dests]

    inverse, *normed = call(
        "prep",
        functools.partial(prep_body, count),
        (1,),
        3,
        [whole((tok_count, width)), whole((1, width))],
        [whole((tok_count, 1))] + [whole((cols, tok_count))] * count,
        [sds((tok_count, 1), f32)] + [sds((cols, tok_count), bf16)] * count,
    )(place, core, chip, tok_rows, norm_gain)
    normed = [normed[0]] + [swap(normed[k], "fsdp", k) for k in dests]

    rows_step = 256
    low = call(
        "low",
        low_body,
        (cols // rows_step,),
        0,
        [pl.BlockSpec((rows_step, kv_cols), lambda i: (i, 0)), anywhere],
        pl.BlockSpec((rows_step, kv_cols), lambda i: (i, 0)),
        sds((cols, kv_cols), bf16),
    )(master_rows, inverse)
    ordered, *spread = call(
        "spread",
        functools.partial(spread_body, count, plan.shape[0], scale),
        (),
        1,
        [resident] * (count + 1),
        [resident] * (count + 1),
        [sds((count * tok_count, kv_cols), bf16)] + [sds((tok_count, cols), bf16)] * count,
        work=10**10,
    )(plan, *cots[::-1], low)
    spread = [spread[0]] + [swap(spread[k], "fsdp", k) for k in dests]

    state = pl.BlockSpec((rows_step, kv_cols), lambda i, *_: (i, 0))
    moment_new, second_new, *rollout_parts, grad_mark = call(
        "grad",
        functools.partial(grad_body, count, head, scale),
        (cols // rows_step,),
        2,
        [pl.BlockSpec((rows_step, tok_count), lambda i, *_: (i, 0))] * count
        + [resident, resident, resident, resident],
        [state, state]
        + [pl.BlockSpec((2 * head, rows_step), lambda i, *_: (0, i))] * count
        + [whole((8, 128))],
        [sds((cols, kv_cols), f32)] * 2 + [sds((2 * head, cols), bf16)] * count + [mark],
        scratch=[
            pltpu.VMEM((rows_step, count * tok_count), bf16),
            pltpu.VMEM((rows_step, kv_cols), bf16),
        ],
        vmem=20,
    )(place, head_owner[0], *normed[::-1], ordered, master_rows, moment_rows, second_rows)

    rollout = ()
    rollout_mark = ()
    for k in (0, 3, 1, 2):
        part = swap(rollout_parts[k], "fsdp", k) if k else rollout_parts[k]
        final = k == 2
        rollout, *rollout_mark = call(
            "place",
            marked_body if final else place_body,
            (1,),
            1,
            [whole((2 * head, cols))] + ([anywhere] if k else []),
            [pl.BlockSpec((2 * head, cols), lambda i, place_ref, k=k: (0, place_ref[0] ^ k))]
            + ([whole((8, 128))] if final else []),
            [sds((2 * head, width), bf16)] + ([mark] if final else []),
            aliases={2: 0} if k else None,
            work=1,
        )(place, part, *([rollout] if k else []))

    def own(name, mine, after):
        (term,) = call(
            name,
            functools.partial(own_body, count, mine),
            (1,),
            2,
            [whole((tok_count, width)), whole((1, width)), whole((tok_count, 1))]
            + [whole((tok_count, cols))] * count
            + [anywhere],
            [whole((half, width))],
            [sds((half, width), bf16)],
        )(place, core, tok_rows, norm_gain, inverse, *spread[::-1], after)
        return term

    give = own("own", False, grad_mark)
    keep = own("keep", True, give)
    got = swap(give, "section", 1)

    def chips(pairs):
        return [(2 * a + c, 2 * b + c) for c in range(2) for a, b in pairs]

    quarter = half // 2
    full, part = whole((half, width)), whole((quarter, width))
    piece = sds((quarter, width), bf16)
    one, two = call("pair", pair_body, (1,), 1, [full, full], [part, part], [piece, piece])(
        chip, keep, got
    )
    one = lax.ppermute(one, "section", chips([(3, 1), (1, 2)]))
    two = lax.ppermute(two, "section", chips([(2, 1), (3, 2)]))
    three, four = call(
        "middle", middle_body, (1,), 1, [full, full, part, part], [part, part], [piece, piece]
    )(chip, keep, got, two, one)
    three = lax.ppermute(three, "section", chips([(1, 0), (2, 1), (3, 2)]))
    four = lax.ppermute(four, "section", chips([(2, 0)]))
    terms = (chip, core, keep, got, two, one, four, three)
    shapes = [full, full, part, part, part, part, anywhere]
    (send,) = call(
        "last",
        functools.partial(last_body, False),
        (1,),
        2,
        shapes,
        [full],
        [sds((half, width), bf16)],
    )(*terms, *rollout_mark)
    other = swap(send, "section", 1)
    (grads,) = call(
        "mine",
        functools.partial(last_body, True),
        (1,),
        2,
        shapes,
        [pl.BlockSpec((half, width), lambda i, chip_ref, core_ref: (core_ref[0], 0))],
        [sds((tok_count, width), bf16)],
    )(*terms, send)
    grads = call(
        "join",
        place_body,
        (1,),
        1,
        [full, anywhere],
        pl.BlockSpec((half, width), lambda i, core_ref: (1 - core_ref[0], 0)),
        sds((tok_count, width), bf16),
        aliases={2: 0},
    )(core, other, grads)
    return (grads[None], moment_new[None], second_new[None], rollout[None])


def choose(*args):
    tokens, cotangents, norm_gain, master, moment, second, head_owner, plan = args
    count, sections = lax.axis_size("fsdp"), lax.axis_size("section")
    tok_count, width = tokens.shape[1:]
    kv_cols, heads = cotangents.shape[2], head_owner.shape[1]
    fits = (
        count == 4
        and sections == 8
        and heads == count
        and plan.shape[0] == 4
        and kv_cols == 2 * heads * 128
        and (width // count) % 256 == 0
        and tok_count % 128 == 0
        and tok_count % (16 * plan.shape[0]) == 0
    )
    return (shards if fits else shards_any)(*args)


def solution(mesh):
    in_specs = (
        P("section", "fsdp", None),
        P("section", "fsdp", None),
        P("section", None),
        P("section", "fsdp", None),
        P("section", "fsdp", None),
        P("section", "fsdp", None),
        P("section", None),
        P(),
    )
    out_specs = (
        P("section", "fsdp", None),
        P("section", "fsdp", None),
        P("section", "fsdp", None),
        P("section", "fsdp", None),
    )
    return jax.shard_map(choose, mesh=mesh, in_specs=in_specs, out_specs=out_specs, check_vma=False)
```

```python
import functools

import jax
import jax.numpy as jnp
from jax import lax
from jax.experimental import pallas as pl
from jax.experimental.pallas import tpu as pltpu
from jax.sharding import PartitionSpec as P

beta_one = 0.9
beta_two = 0.95
bias_one = 1.0 - 0.9**10
bias_two = 1.0 - 0.95**10
adam_eps = 1e-08
learn_rate = 0.02
weight_decay = 0.1
norm_eps = 1e-06

bf16 = jnp.bfloat16
f32 = jnp.float32


def swap(x, axis, k):
    count = lax.axis_size(axis)
    return lax.ppermute(x, axis, [(i, i ^ k) for i in range(count)])


def adam_step(master, moment, second, gradient):
    moment_new = beta_one * moment + (1.0 - beta_one) * gradient
    second_new = beta_two * second + (1.0 - beta_two) * gradient * gradient
    update = moment_new / bias_one / (jnp.sqrt(second_new / bias_two) + adam_eps)
    weights = master - learn_rate * (update + weight_decay * master)
    return (moment_new, second_new, weights)


def plan_rows(cot_rows, plan):
    micro_count = plan.shape[0]
    blocks = cot_rows.reshape(micro_count, -1, cot_rows.shape[-1])
    return jnp.take(blocks, plan, axis=0).reshape(cot_rows.shape)


def suffix_sum(own_term, axis):
    count = lax.axis_size(axis)
    place = lax.axis_index(axis)
    low = own_term.astype(bf16)
    pair = lax.ppermute(low, axis, [(i + 1, i) for i in range(0, count, 2)])
    total = own_term + pair.astype(f32)
    above = jnp.zeros_like(low)
    for z in range(count // 2 - 1, 0, -1):
        got = lax.ppermute(total.astype(bf16), axis, [(2 * z, 2 * z - 2)])
        total = total + got.astype(f32)
        above = above + got
    from_pair = lax.ppermute(above, axis, [(i, i + 1) for i in range(0, count, 2)])
    return jnp.where(place % 2 == 0, total, own_term + from_pair.astype(f32))


def shards_any(tokens, cotangents, norm_gain, master, moment, second, head_owner, plan):
    tok_rows = tokens[0]
    gain_row = norm_gain[0]
    master_rows = master[0]
    owner_row = head_owner[0]
    width = tok_rows.shape[1]
    tok_count = tok_rows.shape[0]
    proj_scale = width ** (-0.5)
    count = lax.axis_size("fsdp")
    place = lax.axis_index("fsdp")
    cols = width // count

    def block_of(x, k):
        return lax.dynamic_slice_in_dim(x, (place ^ k) * cols, cols, axis=-1)

    ordered = plan_rows(cotangents[0], plan)
    all_ordered = [ordered] + [swap(ordered, "fsdp", k) for k in range(1, count)]
    widened = tok_rows.astype(f32)
    inverse = lax.rsqrt(jnp.mean(widened * widened, axis=-1, keepdims=True) + norm_eps)
    normed = (widened * inverse * gain_row).astype(bf16)
    all_normed = [block_of(normed, 0)] + [
        swap(block_of(normed, k), "fsdp", k) for k in range(1, count)
    ]
    low_weights = master_rows.astype(bf16)
    spread = []
    for k in range(count):
        part = (
            jnp.einsum("tc,rc->tr", all_ordered[k], low_weights, preferred_element_type=f32)
            * proj_scale
        )
        spread.append(part if k == 0 else swap(part.astype(bf16), "fsdp", k).astype(f32))

    gradient = (
        jnp.einsum(
            "td,tc->dc",
            jnp.concatenate(all_normed, axis=0),
            jnp.concatenate(all_ordered, axis=0),
            preferred_element_type=f32,
        )
        * proj_scale
    )
    moment_new, second_new, weights = adam_step(master_rows, moment[0], second[0], gradient)
    heads = owner_row.shape[0]
    low_new = weights.astype(bf16).reshape(cols, 2, heads, -1)
    arranged = jnp.take(low_new, owner_row, axis=2).transpose(2, 1, 3, 0).reshape(count, -1, cols)
    rollout = jnp.zeros((arranged.shape[1], width), bf16)
    for k in range(count):
        part = lax.dynamic_index_in_dim(arranged, place ^ k, 0, False)
        if k:
            part = swap(part, "fsdp", k)
        rollout = lax.dynamic_update_slice_in_dim(rollout, part, (place ^ k) * cols, axis=1)

    tok_k = [block_of(tok_rows, k).astype(f32) for k in range(count)]
    scaled = [spread[k] * block_of(gain_row, k) for k in range(count)]
    mean_term = sum(jnp.sum(scaled[k] * tok_k[k], axis=-1, keepdims=True) for k in range(count)) / width
    factor = inverse * inverse * inverse * mean_term
    own_term = jnp.concatenate(
        [inverse * scaled[k] - tok_k[k] * factor for k in range(count)], axis=0
    )
    summed = suffix_sum(own_term, "section").astype(bf16).reshape(count, tok_count, cols)
    input_grads = jnp.zeros((tok_count, width), bf16)
    for k in range(count):
        input_grads = lax.dynamic_update_slice_in_dim(
            input_grads, summed[k], (place ^ k) * cols, axis=1
        )
    return (input_grads[None], moment_new[None], second_new[None], rollout[None])


def call(name, body, grid, prefetch, in_specs, out_specs, out_shape, scratch=(), aliases=None, vmem=16, work=1):
    return pl.pallas_call(
        body,
        grid_spec=pltpu.PrefetchScalarGridSpec(
            num_scalar_prefetch=prefetch,
            grid=grid,
            in_specs=in_specs,
            out_specs=out_specs,
            scratch_shapes=list(scratch),
        ),
        out_shape=out_shape,
        input_output_aliases=aliases or {},
        name=name,
        compiler_params=pltpu.CompilerParams(
            vmem_limit_bytes=vmem * 1024 * 1024,
            dimension_semantics=("arbitrary",) * len(grid),
        ),
        cost_estimate=pl.CostEstimate(flops=work, bytes_accessed=1, transcendentals=0),
    )


def whole(shape):
    return pl.BlockSpec(shape, lambda *_: (0,) * len(shape))


def part_of(place, k, cols):
    return pl.ds(pl.multiple_of((place ^ k) * cols, 128), cols)


def prep_body(count, place_ref, core_ref, chip_ref, tok_ref, gain_ref, inv_ref, *out_refs):
    place = place_ref[0]
    width = tok_ref.shape[1]
    cols = width // count
    total = jnp.zeros((tok_ref.shape[0], 1), f32)
    for k in range(count):
        x = tok_ref[:, k * cols : (k + 1) * cols].astype(f32)
        total = total + jnp.sum(x * x, axis=-1, keepdims=True)
    inverse = lax.rsqrt(total / width + norm_eps)
    inv_ref[...] = inverse
    for k in range(count):
        part = part_of(place, k, cols)
        x = tok_ref[:, part].astype(f32)
        out_refs[k][...] = (x * inverse * gain_ref[:, part]).astype(bf16).T


def low_body(master_ref, _, low_ref):
    low_ref[...] = master_ref[...].astype(bf16)


def spread_body(count, micro, scale, plan_ref, *refs):
    cots, (low_ref, ordered_ref), outs = refs[:count], refs[count : count + 2], refs[count + 2 :]
    rows = cots[0].shape[0]
    size = rows // micro
    for k in range(count):
        for i in range(micro):
            at = pl.multiple_of(plan_ref[i] * size, size)
            ordered_ref[k * rows + i * size : k * rows + (i + 1) * size, :] = cots[k][
                pl.ds(at, size), :
            ]
    step = 256
    for at in range(0, low_ref.shape[0], step):
        product = lax.dot_general(
            ordered_ref[...],
            low_ref[at : at + step, :],
            (((1,), (1,)), ((), ())),
            preferred_element_type=f32,
        )
        for k in range(count):
            outs[k][:, at : at + step] = (product[k * rows : (k + 1) * rows, :] * scale).astype(bf16)


def grad_body(count, head, scale, place_ref, owner_ref, *refs):
    normed, refs = refs[:count], refs[count:]
    ordered_ref, master_ref, moment_ref, second_ref, moment_out, second_out = refs[:6]
    outs, mark_ref, joined, fresh = refs[6 : 6 + count], *refs[6 + count :]
    tok_count = normed[0].shape[1]
    kv_cols = master_ref.shape[1]
    mark_ref[...] = jnp.zeros_like(mark_ref)
    for k in range(count):
        joined[:, k * tok_count : (k + 1) * tok_count] = normed[k][...]
    step = 256
    size = joined.shape[0]
    rows = pl.ds(pl.multiple_of(pl.program_id(0) * size, size), size)
    for at in range(0, kv_cols, step):
        here = slice(at, at + step)
        part = jnp.dot(joined[...], ordered_ref[:, here], preferred_element_type=f32)
        moment_new = beta_one * moment_ref[rows, here] + ((1.0 - beta_one) * scale) * part
        second_new = beta_two * second_ref[rows, here] + (
            ((1.0 - beta_two) * scale * scale) * part
        ) * part
        moment_out[:, here] = moment_new
        second_out[:, here] = second_new
        scaled = second_new * (1.0 / bias_two)
        root = scaled * lax.rsqrt(scaled) + adam_eps
        weights = master_ref[rows, here] * (1.0 - learn_rate * weight_decay) - (
            moment_new * (learn_rate / bias_one)
        ) * pl.reciprocal(root, approx=True)
        fresh[:, here] = weights.astype(bf16)
    for k in range(count):
        owner = owner_ref[place_ref[0] ^ k] * head
        for p in range(2):
            lanes = pl.ds(pl.multiple_of(p * (kv_cols // 2) + owner, head), head)
            outs[k][p * head : (p + 1) * head, :] = fresh[:, lanes].T


def own_body(count, mine, place_ref, core_ref, tok_ref, gain_ref, inv_ref, *refs):
    spread, out_ref = refs[:count][::-1], refs[-1]
    place = place_ref[0]
    core = core_ref[0]
    width = tok_ref.shape[1]
    cols = width // count
    half = tok_ref.shape[0] // 2
    pick = core if mine else 1 - core
    rows = pl.ds(pl.multiple_of(pick * half, half), half)
    inverse = inv_ref[rows, :]
    total = jnp.zeros((half, 1), f32)
    for k in range(count):
        part = part_of(place, k, cols)
        scaled = spread[k][rows, :].astype(f32) * gain_ref[:, part]
        total = total + jnp.sum(
            scaled * tok_ref[rows, part].astype(f32), axis=-1, keepdims=True
        )
    factor = inverse * inverse * inverse * (total / width)
    for k in range(count):
        part = part_of(place, k, cols)
        scaled = spread[k][rows, :].astype(f32) * gain_ref[:, part]
        out_ref[:, part] = (
            inverse * scaled - tok_ref[rows, part].astype(f32) * factor
        ).astype(bf16)


def pair_body(chip_ref, keep_ref, got_ref, one_ref, two_ref):
    z = chip_ref[0]
    half = one_ref.shape[0]
    for out_ref, top in ((one_ref, z == 3), (two_ref, z == 2)):
        rows = pl.ds(pl.multiple_of(jnp.where(top, 0, half), half), half)
        out_ref[...] = (keep_ref[rows, :].astype(f32) + got_ref[rows, :].astype(f32)).astype(bf16)


def middle_body(chip_ref, keep_ref, got_ref, two_ref, one_ref, three_ref, four_ref):
    z = chip_ref[0]
    half = one_ref.shape[0]
    rows = pl.ds(pl.multiple_of(jnp.where(z == 2, half, 0), half), half)
    one = one_ref[...].astype(f32)
    two = two_ref[...].astype(f32)
    mine = keep_ref[rows, :].astype(f32) + got_ref[rows, :].astype(f32) + two
    three_ref[...] = (mine + jnp.where(z == 1, one, 0.0)).astype(bf16)
    four_ref[...] = (mine + one).astype(bf16)


def last_body(mine, chip_ref, core_ref, keep_ref, got_ref, two_ref, one_ref, four_ref, three_ref, _, out_ref):
    z = chip_ref[0]
    lower = (core_ref[0] == 0) == mine
    half = one_ref.shape[0]
    kept, came = (keep_ref, got_ref) if mine else (got_ref, keep_ref)
    for part in range(2):
        rows = slice(part * half, (part + 1) * half)
        one = one_ref[...].astype(f32)
        two = two_ref[...].astype(f32)
        three = three_ref[...].astype(f32)
        if part == 0:
            above = jnp.where(z == 1, one + two, three)
        else:
            four = four_ref[...].astype(f32)
            above = jnp.where(z == 0, four, jnp.where(z == 1, three, two))
        total = kept[rows, :].astype(f32) + above
        both = total + came[rows, :].astype(f32)
        out_ref[rows, :] = jnp.where(lower, both, total).astype(bf16)


def place_body(place_ref, part_ref, *refs):
    refs[-1][...] = part_ref[...]


def marked_body(place_ref, part_ref, _, out_ref, mark_ref):
    out_ref[...] = part_ref[...]
    mark_ref[...] = jnp.zeros_like(mark_ref)


def shards(tokens, cotangents, norm_gain, master, moment, second, head_owner, plan):
    tok_rows, cot_rows = tokens[0], cotangents[0]
    master_rows, moment_rows, second_rows = master[0], moment[0], second[0]
    tok_count, width = tok_rows.shape
    kv_cols = cot_rows.shape[1]
    heads = head_owner.shape[1]
    head = kv_cols // (2 * heads)
    scale = width ** (-0.5)
    count = lax.axis_size("fsdp")
    place = lax.axis_index("fsdp").astype(jnp.int32)[None]
    section = lax.axis_index("section").astype(jnp.int32)
    core, chip = (section & 1)[None], (section >> 1)[None]
    cols = width // count
    half = tok_count // 2
    sds = jax.ShapeDtypeStruct
    dests = range(1, count)
    anywhere = pl.BlockSpec(memory_space=pl.ANY)
    resident = pl.BlockSpec(memory_space=pltpu.VMEM)
    mark = sds((8, 128), f32)

    cots = [cot_rows] + [swap(cot_rows, "fsdp", k) for k in dests]

    inverse, *normed = call(
        "prep",
        functools.partial(prep_body, count),
        (1,),
        3,
        [whole((tok_count, width)), whole((1, width))],
        [whole((tok_count, 1))] + [whole((cols, tok_count))] * count,
        [sds((tok_count, 1), f32)] + [sds((cols, tok_count), bf16)] * count,
    )(place, core, chip, tok_rows, norm_gain)
    normed = [normed[0]] + [swap(normed[k], "fsdp", k) for k in dests]

    rows_step = 256
    low = call(
        "low",
        low_body,
        (cols // rows_step,),
        0,
        [pl.BlockSpec((rows_step, kv_cols), lambda i: (i, 0)), anywhere],
        pl.BlockSpec((rows_step, kv_cols), lambda i: (i, 0)),
        sds((cols, kv_cols), bf16),
    )(master_rows, inverse)
    ordered, *spread = call(
        "spread",
        functools.partial(spread_body, count, plan.shape[0], scale),
        (),
        1,
        [resident] * (count + 1),
        [resident] * (count + 1),
        [sds((count * tok_count, kv_cols), bf16)] + [sds((tok_count, cols), bf16)] * count,
        work=10**10,
    )(plan, *cots, low)
    spread = [spread[0]] + [swap(spread[k], "fsdp", k) for k in dests]

    state = pl.BlockSpec((rows_step, kv_cols), lambda i, *_: (i, 0))
    moment_new, second_new, *rollout_parts, grad_mark = call(
        "grad",
        functools.partial(grad_body, count, head, scale),
        (cols // rows_step,),
        2,
        [pl.BlockSpec((rows_step, tok_count), lambda i, *_: (i, 0))] * count
        + [resident, resident, resident, resident],
        [state, state]
        + [pl.BlockSpec((2 * head, rows_step), lambda i, *_: (0, i))] * count
        + [whole((8, 128))],
        [sds((cols, kv_cols), f32)] * 2 + [sds((2 * head, cols), bf16)] * count + [mark],
        scratch=[
            pltpu.VMEM((rows_step, count * tok_count), bf16),
            pltpu.VMEM((rows_step, kv_cols), bf16),
        ],
        vmem=20,
    )(place, head_owner[0], *normed, ordered, master_rows, moment_rows, second_rows)

    rollout = ()
    rollout_mark = ()
    for k in (0, 3, 1, 2):
        part = swap(rollout_parts[k], "fsdp", k) if k else rollout_parts[k]
        final = k == 2
        rollout, *rollout_mark = call(
            "place",
            marked_body if final else place_body,
            (1,),
            1,
            [whole((2 * head, cols))] + ([anywhere] if k else []),
            [pl.BlockSpec((2 * head, cols), lambda i, place_ref, k=k: (0, place_ref[0] ^ k))]
            + ([whole((8, 128))] if final else []),
            [sds((2 * head, width), bf16)] + ([mark] if final else []),
            aliases={2: 0} if k else None,
            work=1,
        )(place, part, *([rollout] if k else []))

    def own(name, mine, after):
        (term,) = call(
            name,
            functools.partial(own_body, count, mine),
            (1,),
            2,
            [whole((tok_count, width)), whole((1, width)), whole((tok_count, 1))]
            + [whole((tok_count, cols))] * count
            + [anywhere],
            [whole((half, width))],
            [sds((half, width), bf16)],
        )(place, core, tok_rows, norm_gain, inverse, *spread[::-1], after)
        return term

    give = own("own", False, grad_mark)
    keep = own("keep", True, give)
    got = swap(give, "section", 1)

    def chips(pairs):
        return [(2 * a + c, 2 * b + c) for c in range(2) for a, b in pairs]

    quarter = half // 2
    full, part = whole((half, width)), whole((quarter, width))
    piece = sds((quarter, width), bf16)
    one, two = call("pair", pair_body, (1,), 1, [full, full], [part, part], [piece, piece])(
        chip, keep, got
    )
    one = lax.ppermute(one, "section", chips([(3, 1), (1, 2)]))
    two = lax.ppermute(two, "section", chips([(2, 1), (3, 2)]))
    three, four = call(
        "middle", middle_body, (1,), 1, [full, full, part, part], [part, part], [piece, piece]
    )(chip, keep, got, two, one)
    three = lax.ppermute(three, "section", chips([(1, 0), (2, 1), (3, 2)]))
    four = lax.ppermute(four, "section", chips([(2, 0)]))
    terms = (chip, core, keep, got, two, one, four, three)
    shapes = [full, full, part, part, part, part, anywhere]
    (send,) = call(
        "last",
        functools.partial(last_body, False),
        (1,),
        2,
        shapes,
        [full],
        [sds((half, width), bf16)],
    )(*terms, *rollout_mark)
    other = swap(send, "section", 1)
    (grads,) = call(
        "mine",
        functools.partial(last_body, True),
        (1,),
        2,
        shapes,
        [pl.BlockSpec((half, width), lambda i, chip_ref, core_ref: (core_ref[0], 0))],
        [sds((tok_count, width), bf16)],
    )(*terms, send)
    grads = call(
        "join",
        place_body,
        (1,),
        1,
        [full, anywhere],
        pl.BlockSpec((half, width), lambda i, core_ref: (1 - core_ref[0], 0)),
        sds((tok_count, width), bf16),
        aliases={2: 0},
    )(core, other, grads)
    return (grads[None], moment_new[None], second_new[None], rollout[None])


def choose(*args):
    tokens, cotangents, norm_gain, master, moment, second, head_owner, plan = args
    count, sections = lax.axis_size("fsdp"), lax.axis_size("section")
    tok_count, width = tokens.shape[1:]
    kv_cols, heads = cotangents.shape[2], head_owner.shape[1]
    fits = (
        count == 4
        and sections == 8
        and heads == count
        and plan.shape[0] == 4
        and kv_cols == 2 * heads * 128
        and (width // count) % 256 == 0
        and tok_count % 128 == 0
        and tok_count % (16 * plan.shape[0]) == 0
    )
    return (shards if fits else shards_any)(*args)


def solution(mesh):
    in_specs = (
        P("section", "fsdp", None),
        P("section", "fsdp", None),
        P("section", None),
        P("section", "fsdp", None),
        P("section", "fsdp", None),
        P("section", "fsdp", None),
        P("section", None),
        P(),
    )
    out_specs = (
        P("section", "fsdp", None),
        P("section", "fsdp", None),
        P("section", "fsdp", None),
        P("section", "fsdp", None),
    )
    return jax.shard_map(choose, mesh=mesh, in_specs=in_specs, out_specs=out_specs, check_vma=False)
```

```python
import functools

import jax
import jax.numpy as jnp
from jax import lax
from jax.experimental import pallas as pl
from jax.experimental.pallas import tpu as pltpu
from jax.sharding import PartitionSpec as P

beta_one = 0.9
beta_two = 0.95
bias_one = 1.0 - 0.9**10
bias_two = 1.0 - 0.95**10
adam_eps = 1e-08
learn_rate = 0.02
weight_decay = 0.1
norm_eps = 1e-06

bf16 = jnp.bfloat16
f32 = jnp.float32


def swap(x, axis, k):
    count = lax.axis_size(axis)
    return lax.ppermute(x, axis, [(i, i ^ k) for i in range(count)])


def adam_step(master, moment, second, gradient):
    moment_new = beta_one * moment + (1.0 - beta_one) * gradient
    second_new = beta_two * second + (1.0 - beta_two) * gradient * gradient
    update = moment_new / bias_one / (jnp.sqrt(second_new / bias_two) + adam_eps)
    weights = master - learn_rate * (update + weight_decay * master)
    return (moment_new, second_new, weights)


def plan_rows(cot_rows, plan):
    micro_count = plan.shape[0]
    blocks = cot_rows.reshape(micro_count, -1, cot_rows.shape[-1])
    return jnp.take(blocks, plan, axis=0).reshape(cot_rows.shape)


def suffix_sum(own_term, axis):
    count = lax.axis_size(axis)
    place = lax.axis_index(axis)
    low = own_term.astype(bf16)
    pair = lax.ppermute(low, axis, [(i + 1, i) for i in range(0, count, 2)])
    total = own_term + pair.astype(f32)
    above = jnp.zeros_like(low)
    for z in range(count // 2 - 1, 0, -1):
        got = lax.ppermute(total.astype(bf16), axis, [(2 * z, 2 * z - 2)])
        total = total + got.astype(f32)
        above = above + got
    from_pair = lax.ppermute(above, axis, [(i, i + 1) for i in range(0, count, 2)])
    return jnp.where(place % 2 == 0, total, own_term + from_pair.astype(f32))


def shards_any(tokens, cotangents, norm_gain, master, moment, second, head_owner, plan):
    tok_rows = tokens[0]
    gain_row = norm_gain[0]
    master_rows = master[0]
    owner_row = head_owner[0]
    width = tok_rows.shape[1]
    tok_count = tok_rows.shape[0]
    proj_scale = width ** (-0.5)
    count = lax.axis_size("fsdp")
    place = lax.axis_index("fsdp")
    cols = width // count

    def block_of(x, k):
        return lax.dynamic_slice_in_dim(x, (place ^ k) * cols, cols, axis=-1)

    ordered = plan_rows(cotangents[0], plan)
    all_ordered = [ordered] + [swap(ordered, "fsdp", k) for k in range(1, count)]
    widened = tok_rows.astype(f32)
    inverse = lax.rsqrt(jnp.mean(widened * widened, axis=-1, keepdims=True) + norm_eps)
    normed = (widened * inverse * gain_row).astype(bf16)
    all_normed = [block_of(normed, 0)] + [
        swap(block_of(normed, k), "fsdp", k) for k in range(1, count)
    ]
    low_weights = master_rows.astype(bf16)
    spread = []
    for k in range(count):
        part = (
            jnp.einsum("tc,rc->tr", all_ordered[k], low_weights, preferred_element_type=f32)
            * proj_scale
        )
        spread.append(part if k == 0 else swap(part.astype(bf16), "fsdp", k).astype(f32))

    gradient = (
        jnp.einsum(
            "td,tc->dc",
            jnp.concatenate(all_normed, axis=0),
            jnp.concatenate(all_ordered, axis=0),
            preferred_element_type=f32,
        )
        * proj_scale
    )
    moment_new, second_new, weights = adam_step(master_rows, moment[0], second[0], gradient)
    heads = owner_row.shape[0]
    low_new = weights.astype(bf16).reshape(cols, 2, heads, -1)
    arranged = jnp.take(low_new, owner_row, axis=2).transpose(2, 1, 3, 0).reshape(count, -1, cols)
    rollout = jnp.zeros((arranged.shape[1], width), bf16)
    for k in range(count):
        part = lax.dynamic_index_in_dim(arranged, place ^ k, 0, False)
        if k:
            part = swap(part, "fsdp", k)
        rollout = lax.dynamic_update_slice_in_dim(rollout, part, (place ^ k) * cols, axis=1)

    tok_k = [block_of(tok_rows, k).astype(f32) for k in range(count)]
    scaled = [spread[k] * block_of(gain_row, k) for k in range(count)]
    mean_term = sum(jnp.sum(scaled[k] * tok_k[k], axis=-1, keepdims=True) for k in range(count)) / width
    factor = inverse * inverse * inverse * mean_term
    own_term = jnp.concatenate(
        [inverse * scaled[k] - tok_k[k] * factor for k in range(count)], axis=0
    )
    summed = suffix_sum(own_term, "section").astype(bf16).reshape(count, tok_count, cols)
    input_grads = jnp.zeros((tok_count, width), bf16)
    for k in range(count):
        input_grads = lax.dynamic_update_slice_in_dim(
            input_grads, summed[k], (place ^ k) * cols, axis=1
        )
    return (input_grads[None], moment_new[None], second_new[None], rollout[None])


def call(name, body, grid, prefetch, in_specs, out_specs, out_shape, scratch=(), aliases=None, vmem=16, work=1):
    return pl.pallas_call(
        body,
        grid_spec=pltpu.PrefetchScalarGridSpec(
            num_scalar_prefetch=prefetch,
            grid=grid,
            in_specs=in_specs,
            out_specs=out_specs,
            scratch_shapes=list(scratch),
        ),
        out_shape=out_shape,
        input_output_aliases=aliases or {},
        name=name,
        compiler_params=pltpu.CompilerParams(
            vmem_limit_bytes=vmem * 1024 * 1024,
            dimension_semantics=("arbitrary",) * len(grid),
        ),
        cost_estimate=pl.CostEstimate(flops=work, bytes_accessed=1, transcendentals=0),
    )


def whole(shape):
    return pl.BlockSpec(shape, lambda *_: (0,) * len(shape))


def part_of(place, k, cols):
    return pl.ds(pl.multiple_of((place ^ k) * cols, 128), cols)


def prep_body(count, place_ref, core_ref, chip_ref, tok_ref, gain_ref, inv_ref, *out_refs):
    place = place_ref[0]
    width = tok_ref.shape[1]
    cols = width // count
    total = jnp.zeros((tok_ref.shape[0], 1), f32)
    for k in range(count):
        x = tok_ref[:, k * cols : (k + 1) * cols].astype(f32)
        total = total + jnp.sum(x * x, axis=-1, keepdims=True)
    inverse = lax.rsqrt(total / width + norm_eps)
    inv_ref[...] = inverse
    for k in range(count):
        part = part_of(place, k, cols)
        x = tok_ref[:, part].astype(f32)
        out_refs[k][...] = (x * inverse * gain_ref[:, part]).astype(bf16).T


def low_body(master_ref, _, low_ref):
    low_ref[...] = master_ref[...].astype(bf16)


def spread_body(count, micro, scale, plan_ref, *refs):
    cots, (low_ref, ordered_ref), outs = refs[:count][::-1], refs[count : count + 2], refs[count + 2 :]
    rows = cots[0].shape[0]
    size = rows // micro
    for k in range(count):
        for i in range(micro):
            at = pl.multiple_of(plan_ref[i] * size, size)
            ordered_ref[k * rows + i * size : k * rows + (i + 1) * size, :] = cots[k][
                pl.ds(at, size), :
            ]
    step = 256
    for at in range(0, low_ref.shape[0], step):
        product = lax.dot_general(
            ordered_ref[...],
            low_ref[at : at + step, :],
            (((1,), (1,)), ((), ())),
            preferred_element_type=f32,
        )
        for k in range(count):
            outs[k][:, at : at + step] = (product[k * rows : (k + 1) * rows, :] * scale).astype(bf16)


def grad_body(count, head, scale, place_ref, owner_ref, *refs):
    normed, refs = refs[:count][::-1], refs[count:]
    ordered_ref, master_ref, moment_ref, second_ref, moment_out, second_out = refs[:6]
    outs, mark_ref, joined, fresh = refs[6 : 6 + count], *refs[6 + count :]
    tok_count = normed[0].shape[1]
    kv_cols = master_ref.shape[1]
    mark_ref[...] = jnp.zeros_like(mark_ref)
    for k in range(count):
        joined[:, k * tok_count : (k + 1) * tok_count] = normed[k][...]
    step = 256
    size = joined.shape[0]
    rows = pl.ds(pl.multiple_of(pl.program_id(0) * size, size), size)
    for at in range(0, kv_cols, step):
        here = slice(at, at + step)
        part = jnp.dot(joined[...], ordered_ref[:, here], preferred_element_type=f32)
        moment_new = beta_one * moment_ref[rows, here] + ((1.0 - beta_one) * scale) * part
        second_new = beta_two * second_ref[rows, here] + (
            ((1.0 - beta_two) * scale * scale) * part
        ) * part
        moment_out[:, here] = moment_new
        second_out[:, here] = second_new
        scaled = second_new * (1.0 / bias_two)
        root = scaled * lax.rsqrt(scaled) + adam_eps
        weights = master_ref[rows, here] * (1.0 - learn_rate * weight_decay) - (
            moment_new * (learn_rate / bias_one)
        ) * pl.reciprocal(root, approx=True)
        fresh[:, here] = weights.astype(bf16)
    for k in range(count):
        owner = owner_ref[place_ref[0] ^ k] * head
        for p in range(2):
            lanes = pl.ds(pl.multiple_of(p * (kv_cols // 2) + owner, head), head)
            outs[k][p * head : (p + 1) * head, :] = fresh[:, lanes].T


def own_body(count, mine, place_ref, core_ref, tok_ref, gain_ref, inv_ref, *refs):
    spread, out_ref = refs[:count], refs[-1]
    place = place_ref[0]
    core = core_ref[0]
    width = tok_ref.shape[1]
    cols = width // count
    half = tok_ref.shape[0] // 2
    pick = core if mine else 1 - core
    rows = pl.ds(pl.multiple_of(pick * half, half), half)
    inverse = inv_ref[rows, :]
    total = jnp.zeros((half, 1), f32)
    for k in range(count):
        part = part_of(place, k, cols)
        scaled = spread[k][rows, :].astype(f32) * gain_ref[:, part]
        total = total + jnp.sum(
            scaled * tok_ref[rows, part].astype(f32), axis=-1, keepdims=True
        )
    factor = inverse * inverse * inverse * (total / width)
    for k in range(count):
        part = part_of(place, k, cols)
        scaled = spread[k][rows, :].astype(f32) * gain_ref[:, part]
        out_ref[:, part] = (
            inverse * scaled - tok_ref[rows, part].astype(f32) * factor
        ).astype(bf16)


def pair_body(chip_ref, keep_ref, got_ref, one_ref, two_ref):
    z = chip_ref[0]
    half = one_ref.shape[0]
    for out_ref, top in ((one_ref, z == 3), (two_ref, z == 2)):
        rows = pl.ds(pl.multiple_of(jnp.where(top, 0, half), half), half)
        out_ref[...] = (keep_ref[rows, :].astype(f32) + got_ref[rows, :].astype(f32)).astype(bf16)


def middle_body(chip_ref, keep_ref, got_ref, two_ref, one_ref, three_ref, four_ref):
    z = chip_ref[0]
    half = one_ref.shape[0]
    rows = pl.ds(pl.multiple_of(jnp.where(z == 2, half, 0), half), half)
    one = one_ref[...].astype(f32)
    two = two_ref[...].astype(f32)
    mine = keep_ref[rows, :].astype(f32) + got_ref[rows, :].astype(f32) + two
    three_ref[...] = (mine + jnp.where(z == 1, one, 0.0)).astype(bf16)
    four_ref[...] = (mine + one).astype(bf16)


def last_body(mine, chip_ref, core_ref, keep_ref, got_ref, two_ref, one_ref, four_ref, three_ref, _, out_ref):
    z = chip_ref[0]
    lower = (core_ref[0] == 0) == mine
    half = one_ref.shape[0]
    kept, came = (keep_ref, got_ref) if mine else (got_ref, keep_ref)
    for part in range(2):
        rows = slice(part * half, (part + 1) * half)
        one = one_ref[...].astype(f32)
        two = two_ref[...].astype(f32)
        three = three_ref[...].astype(f32)
        if part == 0:
            above = jnp.where(z == 1, one + two, three)
        else:
            four = four_ref[...].astype(f32)
            above = jnp.where(z == 0, four, jnp.where(z == 1, three, two))
        total = kept[rows, :].astype(f32) + above
        both = total + came[rows, :].astype(f32)
        out_ref[rows, :] = jnp.where(lower, both, total).astype(bf16)


def place_body(place_ref, part_ref, *refs):
    refs[-1][...] = part_ref[...]


def marked_body(place_ref, part_ref, _, out_ref, mark_ref):
    out_ref[...] = part_ref[...]
    mark_ref[...] = jnp.zeros_like(mark_ref)


def shards(tokens, cotangents, norm_gain, master, moment, second, head_owner, plan):
    tok_rows, cot_rows = tokens[0], cotangents[0]
    master_rows, moment_rows, second_rows = master[0], moment[0], second[0]
    tok_count, width = tok_rows.shape
    kv_cols = cot_rows.shape[1]
    heads = head_owner.shape[1]
    head = kv_cols // (2 * heads)
    scale = width ** (-0.5)
    count = lax.axis_size("fsdp")
    place = lax.axis_index("fsdp").astype(jnp.int32)[None]
    section = lax.axis_index("section").astype(jnp.int32)
    core, chip = (section & 1)[None], (section >> 1)[None]
    cols = width // count
    half = tok_count // 2
    sds = jax.ShapeDtypeStruct
    dests = range(1, count)
    anywhere = pl.BlockSpec(memory_space=pl.ANY)
    resident = pl.BlockSpec(memory_space=pltpu.VMEM)
    mark = sds((8, 128), f32)

    cots = [cot_rows] + [swap(cot_rows, "fsdp", k) for k in dests]

    inverse, *normed = call(
        "prep",
        functools.partial(prep_body, count),
        (1,),
        3,
        [whole((tok_count, width)), whole((1, width))],
        [whole((tok_count, 1))] + [whole((cols, tok_count))] * count,
        [sds((tok_count, 1), f32)] + [sds((cols, tok_count), bf16)] * count,
    )(place, core, chip, tok_rows, norm_gain)
    normed = [normed[0]] + [swap(normed[k], "fsdp", k) for k in dests]

    rows_step = 256
    low = call(
        "low",
        low_body,
        (cols // rows_step,),
        0,
        [pl.BlockSpec((rows_step, kv_cols), lambda i: (i, 0)), anywhere],
        pl.BlockSpec((rows_step, kv_cols), lambda i: (i, 0)),
        sds((cols, kv_cols), bf16),
    )(master_rows, inverse)
    ordered, *spread = call(
        "spread",
        functools.partial(spread_body, count, plan.shape[0], scale),
        (),
        1,
        [resident] * (count + 1),
        [resident] * (count + 1),
        [sds((count * tok_count, kv_cols), bf16)] + [sds((tok_count, cols), bf16)] * count,
        work=10**10,
    )(plan, *cots[::-1], low)
    spread = [spread[0]] + [swap(spread[k], "fsdp", k) for k in dests]

    state = pl.BlockSpec((rows_step, kv_cols), lambda i, *_: (i, 0))
    moment_new, second_new, *rollout_parts, grad_mark = call(
        "grad",
        functools.partial(grad_body, count, head, scale),
        (cols // rows_step,),
        2,
        [pl.BlockSpec((rows_step, tok_count), lambda i, *_: (i, 0))] * count
        + [resident, resident, resident, resident],
        [state, state]
        + [pl.BlockSpec((2 * head, rows_step), lambda i, *_: (0, i))] * count
        + [whole((8, 128))],
        [sds((cols, kv_cols), f32)] * 2 + [sds((2 * head, cols), bf16)] * count + [mark],
        scratch=[
            pltpu.VMEM((rows_step, count * tok_count), bf16),
            pltpu.VMEM((rows_step, kv_cols), bf16),
        ],
        vmem=20,
    )(place, head_owner[0], *normed[::-1], ordered, master_rows, moment_rows, second_rows)

    rollout = ()
    rollout_mark = ()
    for k in (0, 3, 1, 2):
        part = swap(rollout_parts[k], "fsdp", k) if k else rollout_parts[k]
        final = k == 2
        rollout, *rollout_mark = call(
            "place",
            marked_body if final else place_body,
            (1,),
            1,
            [whole((2 * head, cols))] + ([anywhere] if k else []),
            [pl.BlockSpec((2 * head, cols), lambda i, place_ref, k=k: (0, place_ref[0] ^ k))]
            + ([whole((8, 128))] if final else []),
            [sds((2 * head, width), bf16)] + ([mark] if final else []),
            aliases={2: 0} if k else None,
            work=1,
        )(place, part, *([rollout] if k else []))

    def own(name, mine, after):
        (term,) = call(
            name,
            functools.partial(own_body, count, mine),
            (1,),
            2,
            [whole((tok_count, width)), whole((1, width)), whole((tok_count, 1))]
            + [whole((tok_count, cols))] * count
            + [anywhere],
            [whole((half, width))],
            [sds((half, width), bf16)],
        )(place, core, tok_rows, norm_gain, inverse, *spread, after)
        return term

    give = own("own", False, grad_mark)
    keep = own("keep", True, give)
    got = swap(give, "section", 1)

    def chips(pairs):
        return [(2 * a + c, 2 * b + c) for c in range(2) for a, b in pairs]

    quarter = half // 2
    full, part = whole((half, width)), whole((quarter, width))
    piece = sds((quarter, width), bf16)
    one, two = call("pair", pair_body, (1,), 1, [full, full], [part, part], [piece, piece])(
        chip, keep, got
    )
    one = lax.ppermute(one, "section", chips([(3, 1), (1, 2)]))
    two = lax.ppermute(two, "section", chips([(2, 1), (3, 2)]))
    three, four = call(
        "middle",
        middle_body,
        (1,),
        1,
        [full, full, part, part],
        [part, part],
        [piece, piece],
        work=10**6,
    )(chip, keep, got, two, one)
    three = lax.ppermute(three, "section", chips([(1, 0), (2, 1), (3, 2)]))
    four = lax.ppermute(four, "section", chips([(2, 0)]))
    terms = (chip, core, keep, got, two, one, four, three)
    shapes = [full, full, part, part, part, part, anywhere]
    (send,) = call(
        "last",
        functools.partial(last_body, False),
        (1,),
        2,
        shapes,
        [full],
        [sds((half, width), bf16)],
    )(*terms, *rollout_mark)
    other = swap(send, "section", 1)
    (grads,) = call(
        "mine",
        functools.partial(last_body, True),
        (1,),
        2,
        shapes,
        [pl.BlockSpec((half, width), lambda i, chip_ref, core_ref: (core_ref[0], 0))],
        [sds((tok_count, width), bf16)],
    )(*terms, send)
    grads = call(
        "join",
        place_body,
        (1,),
        1,
        [full, anywhere],
        pl.BlockSpec((half, width), lambda i, core_ref: (1 - core_ref[0], 0)),
        sds((tok_count, width), bf16),
        aliases={2: 0},
    )(core, other, grads)
    return (grads[None], moment_new[None], second_new[None], rollout[None])


def choose(*args):
    tokens, cotangents, norm_gain, master, moment, second, head_owner, plan = args
    count, sections = lax.axis_size("fsdp"), lax.axis_size("section")
    tok_count, width = tokens.shape[1:]
    kv_cols, heads = cotangents.shape[2], head_owner.shape[1]
    fits = (
        count == 4
        and sections == 8
        and heads == count
        and plan.shape[0] == 4
        and kv_cols == 2 * heads * 128
        and (width // count) % 256 == 0
        and tok_count % 128 == 0
        and tok_count % (16 * plan.shape[0]) == 0
    )
    return (shards if fits else shards_any)(*args)


def solution(mesh):
    in_specs = (
        P("section", "fsdp", None),
        P("section", "fsdp", None),
        P("section", None),
        P("section", "fsdp", None),
        P("section", "fsdp", None),
        P("section", "fsdp", None),
        P("section", None),
        P(),
    )
    out_specs = (
        P("section", "fsdp", None),
        P("section", "fsdp", None),
        P("section", "fsdp", None),
        P("section", "fsdp", None),
    )
    return jax.shard_map(choose, mesh=mesh, in_specs=in_specs, out_specs=out_specs, check_vma=False)
```
